32 devices in a mesh: groups: 2 (over x), freq: 16 (over z, y, core).
Axes of the slice: x: 2, y: 2, z: 4, core: 2. Of those that a mesh axis runs over, the one named last changes fastest.
Arguments:
- features: bfloat16 [32, 64, 192], P('groups', 'freq'), parts along dimension 0, may hold values from -6 to 6
- spectrum: bfloat16 [32, 64, 192], P('groups', 'freq'), parts along dimension 0, may hold values from -6 to 6
- cotangent: bfloat16 [32, 64, 192], P('groups', 'freq'), parts along dimension 0, may hold values from -6 to 6
- w_first: bfloat16 [64, 8], P('freq'), may hold values from -2 to 2
- w_second: bfloat16 [64, 8], P('freq'), may hold values from -2 to 2
- w_in: bfloat16 [192, 384], replicated, may hold values from -0.4375 to 0.4375
- w_out: bfloat16 [384, 192], replicated, may hold values from -0.3125 to 0.3125
Outputs:
- enhanced: bfloat16 [32, 64, 192], P('groups', 'freq'), parts along dimension 0
- grad_first: float32 [64, 16], P('freq', 'groups'), parts along dimension 1
- grad_second: float32 [64, 16], P('freq', 'groups'), parts along dimension 1
- grad_w_in: float32 [384, 384], P('groups'), parts along dimension 0
- grad_w_out: float32 [768, 192], P('groups'), parts along dimension 0
The draws below stay inside these ranges and needn't reach their ends.
There are 2 independent parts, one for each index of `groups`. The reference program is written for one: setup_inputs(seed, part) draws one part's arguments, and reference() takes and returns one part's arrays. A program takes and returns all parts, laid end to end along the dimension named above; an argument that names none is the same for every part. Nothing has to cross between parts.
All inputs are finite; a program needn't handle non-finite values.
Results may differ from the reference program's by a relative error of at most 0.0079.
Values may be sent and summed in bfloat16 or wider, within the bound.
No kernel may reach another device: no remote copies, remote signals or barrier semaphores. Data moves between devices by JAX's collectives and lax.ppermute only.
A program may use at most 64 MiB of HBM per device.

```python
import math
import jax
import jax.numpy as jnp

FRAMES = 16
C = 192
HID = 384
BLK = 8
BINS = 64


def block_scale(rng, dims, shards, smallest, top_value):
    def one(axis_at, shards_of):
        steps = jax.random.uniform(jax.random.fold_in(jax.random.fold_in(rng, 6), axis_at), (shards_of,), jnp.float32, smallest / len(shards), top_value / len(shards))
        return jnp.repeat(jnp.exp(steps), dims[axis_at] // shards_of).reshape((-1,) + (1,) * (len(dims) - axis_at - 1))

    gain = one(*shards[0])
    for cut in shards[1:]:
        gain = gain * one(*cut)
    return gain


def scatter_about(key, extent, spread, reach, cuts=(), kind=jnp.bfloat16):
    drawn = jax.random.normal(key, extent, jnp.float32) * spread
    if len(cuts) > 0:
        drawn = block_scale(key, extent, cuts, -0.22, 0.18) * drawn
    return jnp.clip(drawn, min=-reach, max=reach).astype(kind)


def setup_inputs(seed: int = 0, part: int = 0) -> dict:
    splits = jax.random.split(jax.random.key(seed), 8)
    part_splits = jax.random.split(jax.random.fold_in(splits[7], part), 8)
    return {
        "features": scatter_about(part_splits[0], (FRAMES, BINS, C), 1.0, 6.0, ((1, 16),)),
        "spectrum": scatter_about(part_splits[1], (FRAMES, BINS, C), 1.0, 6.0, ((1, 16),)),
        "cotangent": scatter_about(part_splits[2], (FRAMES, BINS, C), 1.0, 6.0, ((1, 16),)),
        "w_first": scatter_about(splits[3], (BINS, BLK), BLK ** -0.5, 2.0, ((0, 16),)),
        "w_second": scatter_about(splits[4], (BINS, BLK), BLK ** -0.5, 2.0, ((0, 16),)),
        "w_in": scatter_about(splits[5], (C, HID), C ** -0.5, 0.4375),
        "w_out": scatter_about(splits[6], (HID, C), HID ** -0.5, 0.3125),
    }


gelu_coef = math.sqrt(2.0 / math.pi)

def gelu_pair(pre_act):
    tanh_arg = gelu_coef * (pre_act + 0.044715 * pre_act * pre_act * pre_act)
    tanh_val = jnp.tanh(tanh_arg)
    gelu_out = 0.5 * pre_act * (1.0 + tanh_val)
    gelu_slope = 0.5 * (1.0 + tanh_val) + 0.5 * pre_act * (1.0 - tanh_val * tanh_val) * gelu_coef * (1.0 + 3.0 * 0.044715 * pre_act * pre_act)
    return (gelu_out, gelu_slope)

def reference(features, spectrum, cotangent, w_first, w_second, w_in, w_out):
    half_c = C // 2
    x_four = features.reshape(FRAMES, BLK, BLK, C).astype(jnp.float32)
    first_w = w_first.reshape(BLK, BLK, BLK).astype(jnp.float32)
    second_w = w_second.reshape(BLK, BLK, BLK).astype(jnp.float32)
    first = jnp.einsum('fabc,abp->fapc', x_four, first_w).astype(jnp.bfloat16)
    spectral = jnp.einsum('fapc,paq->fpqc', first.astype(jnp.float32), second_w).astype(jnp.bfloat16)
    flat_rows = spectral.reshape(FRAMES * BINS, C)
    pre_act = jnp.dot(flat_rows, w_in, preferred_element_type=jnp.float32)
    gelu_out, gelu_slope = gelu_pair(pre_act)
    hidden = gelu_out.astype(jnp.bfloat16)
    spectral_mask = (flat_rows.astype(jnp.float32) + jnp.dot(hidden, w_out, preferred_element_type=jnp.float32)).astype(jnp.bfloat16)
    mask_f = spectral_mask.reshape(FRAMES, BINS, C).astype(jnp.float32)
    spec_f = spectrum.astype(jnp.float32)
    mask_re, mask_im = (mask_f[..., :half_c], mask_f[..., half_c:])
    spec_re, spec_im = (spec_f[..., :half_c], spec_f[..., half_c:])
    enhanced = jnp.concatenate([spec_re * mask_re - spec_im * mask_im, spec_re * mask_im + spec_im * mask_re], -1).astype(jnp.bfloat16)
    loss_scale = jnp.float32(1.0) / jnp.sqrt(jnp.float32(FRAMES * BINS))
    grad_f = cotangent.astype(jnp.float32) * loss_scale
    grad_re, grad_im = (grad_f[..., :half_c], grad_f[..., half_c:])
    dmask = jnp.concatenate([grad_re * spec_re + grad_im * spec_im, grad_im * spec_re - grad_re * spec_im], -1).astype(jnp.bfloat16)
    dmask = dmask.reshape(FRAMES * BINS, C)
    dact = jnp.dot(dmask, w_out.T, preferred_element_type=jnp.float32)
    dpre = (dact * gelu_slope).astype(jnp.bfloat16)
    grad_w_out = jnp.dot(hidden.T, dmask, preferred_element_type=jnp.float32)
    grad_w_in = jnp.dot(flat_rows.T, dpre, preferred_element_type=jnp.float32)
    dspectral = (dmask.astype(jnp.float32) + jnp.dot(dpre, w_in.T, preferred_element_type=jnp.float32)).astype(jnp.bfloat16)
    dspectral = dspectral.reshape(FRAMES, BLK, BLK, C).astype(jnp.float32)
    dfirst = jnp.einsum('fpqc,paq->fapc', dspectral, second_w).astype(jnp.bfloat16)
    grad_second = jnp.einsum('fapc,fpqc->paq', first.astype(jnp.float32), dspectral).reshape(BINS, BLK)
    grad_first = jnp.einsum('fabc,fapc->abp', x_four, dfirst.astype(jnp.float32)).reshape(BINS, BLK)
    return (enhanced, grad_first, grad_second, grad_w_in, grad_w_out)
```

```python
import functools
import math

import jax
import jax.numpy as jnp
from jax import lax
from jax.experimental import pallas as pl
from jax.experimental.pallas import tpu as pltpu
from jax.sharding import PartitionSpec as P

gelu_coef = math.sqrt(2.0 / math.pi)


def swapped(value, axis, distance):
    mask = 2**distance
    pairs = [(source, source ^ mask) for source in range(lax.axis_size(axis))]
    return lax.ppermute(value, axis, pairs)


def gelu_pair(pre_act):
    tanh_arg = gelu_coef * (pre_act + 0.044715 * pre_act * pre_act * pre_act)
    tanh_val = jnp.tanh(tanh_arg)
    gelu_out = 0.5 * pre_act * (1.0 + tanh_val)
    gelu_slope = 0.5 * (1.0 + tanh_val) + 0.5 * pre_act * (
        1.0 - tanh_val * tanh_val
    ) * gelu_coef * (1.0 + 3.0 * 0.044715 * pre_act * pre_act)
    return (gelu_out, gelu_slope)


def spread_back(dfirst_two, features):
    frames, own_bins, channels = features.shape
    block = dfirst_two.shape[0]
    quarter = frames // 4
    devices = 2 * block
    send_back = jnp.broadcast_to(dfirst_two[:, None], (block, 2, 2, quarter, channels)).reshape(
        devices, 2 * quarter * channels
    )
    back_rows = lax.all_to_all(send_back, "freq", split_axis=0, concat_axis=0, tiled=True).reshape(
        block, 2, 2, quarter, channels
    )
    by_quarter_x = features.reshape(2, 2, quarter, own_bins, channels)
    return jnp.einsum(
        "hgtbc,pghtc->bp", by_quarter_x, back_rows, preferred_element_type=jnp.float32
    )


def split_rows(features, spectrum, cotangent, w_first, w_second, w_in, w_out):
    frames, own_bins, channels = features.shape
    block = w_first.shape[1]
    quarter = frames // 4
    half_c = channels // 2
    devices = lax.axis_size("freq")
    parity = lax.axis_index("freq") % 2
    lower_side = parity == 0

    def join_halves(mine, theirs, axis):
        return jnp.where(
            lower_side, jnp.concatenate([mine, theirs], axis), jnp.concatenate([theirs, mine], axis)
        )

    got_second = swapped(w_second, "freq", 0)
    full_second = join_halves(w_second, got_second, 0)
    by_quarter = features.reshape(2, 2, quarter, own_bins, channels)
    partials = jnp.einsum(
        "hgtbc,bp->pghtc", by_quarter, w_first, preferred_element_type=jnp.float32
    )
    partials = partials.reshape(devices, 2 * quarter * channels)
    arrived = lax.all_to_all(partials, "freq", split_axis=0, concat_axis=0, tiled=True)
    first_two = arrived.reshape(block, 2, 2, quarter, channels).sum(axis=1).astype(jnp.bfloat16)
    spectral = jnp.einsum(
        "ahtc,aq->htqc", first_two, full_second, preferred_element_type=jnp.float32
    ).astype(jnp.bfloat16)
    flat_rows = spectral.reshape(-1, channels)
    pre_act = jnp.dot(flat_rows, w_in, preferred_element_type=jnp.float32)
    gelu_out, gelu_slope = gelu_pair(pre_act)
    hidden = gelu_out.astype(jnp.bfloat16)
    spectral_mask = (
        flat_rows.astype(jnp.float32) + jnp.dot(hidden, w_out, preferred_element_type=jnp.float32)
    ).astype(jnp.bfloat16)
    spectral_mask = spectral_mask.reshape(2, quarter, block, channels)
    send_mask = lax.dynamic_slice_in_dim(spectral_mask, (1 - parity) * own_bins, own_bins, 2)
    keep_mask = lax.dynamic_slice_in_dim(spectral_mask, parity * own_bins, own_bins, 2)
    got_mask = swapped(send_mask, "freq", 0)
    full_mask = jnp.where(
        lower_side, jnp.stack([keep_mask, got_mask], 1), jnp.stack([got_mask, keep_mask], 1)
    )
    mask_f = full_mask.reshape(frames, own_bins, channels).astype(jnp.float32)
    spec_f = spectrum.astype(jnp.float32)
    mask_re, mask_im = (mask_f[..., :half_c], mask_f[..., half_c:])
    spec_re, spec_im = (spec_f[..., :half_c], spec_f[..., half_c:])
    enhanced = jnp.concatenate(
        [spec_re * mask_re - spec_im * mask_im, spec_re * mask_im + spec_im * mask_re], -1
    ).astype(jnp.bfloat16)
    loss_scale = jnp.float32(1.0) / jnp.sqrt(jnp.float32(frames * devices * own_bins))
    grad_f = cotangent.astype(jnp.float32) * loss_scale
    grad_re, grad_im = (grad_f[..., :half_c], grad_f[..., half_c:])
    dmask = jnp.concatenate(
        [grad_re * spec_re + grad_im * spec_im, grad_im * spec_re - grad_re * spec_im], -1
    ).astype(jnp.bfloat16)
    dmask = dmask.reshape(2, 2, quarter, own_bins, channels)
    send_dmask = lax.dynamic_index_in_dim(dmask, 1 - parity, 1, keepdims=False)
    keep_dmask = lax.dynamic_index_in_dim(dmask, parity, 1, keepdims=False)
    got_dmask = swapped(send_dmask, "freq", 0)
    dmask_rows = join_halves(keep_dmask, got_dmask, 2).reshape(-1, channels)
    dact = jnp.dot(dmask_rows, w_out.T, preferred_element_type=jnp.float32)
    dpre = (dact * gelu_slope).astype(jnp.bfloat16)
    part_out = jnp.dot(hidden.T, dmask_rows, preferred_element_type=jnp.float32)
    part_in = jnp.dot(flat_rows.T, dpre, preferred_element_type=jnp.float32)
    grad_w_in, grad_w_out = lax.psum((part_in, part_out), "freq")
    dspectral = (
        dmask_rows.astype(jnp.float32) + jnp.dot(dpre, w_in.T, preferred_element_type=jnp.float32)
    ).astype(jnp.bfloat16)
    dspectral = dspectral.reshape(2, quarter, block, channels)
    dfirst_two = jnp.einsum(
        "htqc,aq->ahtc", dspectral, full_second, preferred_element_type=jnp.float32
    ).astype(jnp.bfloat16)
    second_part = jnp.einsum(
        "ahtc,htqc->aq", first_two, dspectral, preferred_element_type=jnp.float32
    )
    second_part = second_part.reshape(2, own_bins, block)
    got_part = swapped(
        lax.dynamic_index_in_dim(second_part, 1 - parity, 0, keepdims=False), "freq", 0
    )
    grad_second = lax.dynamic_index_in_dim(second_part, parity, 0, keepdims=False) + got_part
    grad_first = spread_back(dfirst_two, features)
    return (enhanced, grad_first, grad_second, grad_w_in, grad_w_out)


f32, bf16 = jnp.float32, jnp.bfloat16
NN = (((1,), (0,)), ((), ()))
NT = (((1,), (1,)), ((), ()))
TN = (((0,), (0,)), ((), ()))
LANES = 128
W_ROWS = 16


def mul(a, b, dims=NN):
    return lax.dot_general(a, b, dims, preferred_element_type=f32)


def mul_f32(a, b):
    return lax.dot_general(a, b, NN, precision=lax.Precision.HIGHEST, preferred_element_type=f32)


def iota(shape, dim):
    return lax.broadcasted_iota(jnp.int32, shape, dim)


def pack_rows(rows):
    half = rows.shape[0] // 2
    low, high = rows[:half], rows[half:]
    rest = jnp.concatenate([low[:, LANES:], high[:, LANES:]], 1)
    return low[:, :LANES], high[:, :LANES], rest


def pack_kernel(x_ref, s_ref, c_ref, w1_ref, w2_ref, px_ref, pd_ref, *, scale):
    frames, bins, channels = x_ref.shape
    rows = frames * bins
    half = rows // 2
    half_c = channels // 2
    block = w1_ref.shape[1]

    for t, part in enumerate(pack_rows(x_ref[...].astype(f32).reshape(rows, channels))):
        px_ref[t * half : (t + 1) * half, :] = part.astype(bf16)
    weights = jnp.concatenate([w1_ref[...].astype(f32), w2_ref[...].astype(f32)], 1)
    weights = jnp.concatenate([weights, jnp.zeros((bins, LANES - 2 * block), f32)], 1)
    weights = jnp.concatenate([weights, jnp.zeros((W_ROWS - bins, LANES), f32)], 0)
    px_ref[3 * half :, :] = weights.astype(bf16)

    spec = s_ref[...].astype(f32).reshape(rows, channels)
    grad = c_ref[...].astype(f32).reshape(rows, channels) * scale
    spec_re, spec_im = spec[:, :half_c], spec[:, half_c:]
    grad_re, grad_im = grad[:, :half_c], grad[:, half_c:]
    dmask = jnp.concatenate(
        [grad_re * spec_re + grad_im * spec_im, grad_im * spec_re - grad_re * spec_im], 1
    )
    for t, part in enumerate(pack_rows(dmask)):
        pd_ref[t * half : (t + 1) * half, :] = part.astype(bf16)


def main_kernel(
    gx_ref, gd_ref, s_ref, w_in_ref, w_out_ref,
    enh_ref, g1_ref, g2_ref, gwi_ref, gwo_ref,
    sp_ref, dm_ref, dsp_ref, *, chunk,
):
    frames, bins, channels = s_ref.shape
    block = g1_ref.shape[1]
    half_f = frames // 2
    half_c = channels // 2
    own = half_f * bins
    devices = gx_ref.shape[0] // (3 * own + W_ROWS)
    rows = devices * own
    me = lax.axis_index("freq")
    chip, side = me >> 1, (me & 1) * bins
    per_block = 2 * own

    def block_of(r):
        return r // per_block

    def place_of(r):
        return ((r // own) & 1) * bins + (r & (bins - 1))

    def frame_of(r):
        return (r // bins) & (half_f - 1)

    def gathered(ref, per_device):
        tiles = [
            jnp.concatenate(
                [ref[j * per_device + t * own : j * per_device + (t + 1) * own, :] for j in range(devices)], 0
            )
            for t in range(3)
        ]
        return tiles

    def unpacked(low, high, rest):
        split = channels - LANES
        return (
            jnp.concatenate([low, rest[:, :split]], 1),
            jnp.concatenate([high, rest[:, split:]], 1),
        )

    per_x = 3 * own + W_ROWS
    x_tiles = gathered(gx_ref, per_x)
    weights = jnp.concatenate(
        [gx_ref[j * per_x + 3 * own : (j + 1) * per_x, :] for j in range(devices)], 0
    )
    w_rows = devices * W_ROWS

    w_at = iota((rows, w_rows), 1)
    w_ok = (w_at & (W_ROWS - 1)) < bins
    w_block = w_at // (2 * W_ROWS)
    w_place = ((w_at // W_ROWS) & 1) * bins + (w_at & (W_ROWS - 1))
    r_at = iota((rows, w_rows), 0)
    lane = iota((rows, LANES), 1)
    r_lane = iota((rows, LANES), 0)
    q_at = iota((w_rows, rows), 0)
    q_place = ((q_at // W_ROWS) & 1) * bins + (q_at & (W_ROWS - 1))
    q_block = q_at // (2 * W_ROWS)
    q_row = iota((w_rows, rows), 1)
    m_row, m_col = iota((rows, rows), 0), iota((rows, rows), 1)
    same_frame = frame_of(m_row) == frame_of(m_col)

    def onehot(cond):
        return cond.astype(f32).astype(bf16)

    pick1 = onehot(lane == place_of(r_lane))
    of_row = mul(pick1, weights, NT)
    spread = onehot((q_place == place_of(q_row)) & (q_block == block_of(q_row)))
    mix1 = mul(
        jnp.where(w_ok & (w_block == block_of(r_at)), of_row, 0.0).astype(bf16), spread
    )
    mix1 = jnp.where(same_frame, mix1, 0.0).astype(bf16)

    pick2 = onehot(lane == block + (place_of(r_lane) ^ side))
    of_row = mul(pick2, weights, NT)
    spread = onehot(q_place == (block_of(q_row) ^ chip ^ side))
    mix2 = mul(
        jnp.where(w_ok & (w_block == block_of(r_at)), of_row, 0.0).astype(bf16), spread
    )
    mix2 = jnp.where(same_frame & (place_of(m_col) == (block_of(m_row) ^ chip)), mix2, 0.0).astype(bf16)

    packed_x = jnp.concatenate(x_tiles, 1)
    first = mul(mix1, packed_x).astype(bf16)
    spectral = mul(mix2, first).astype(bf16)
    cut = lambda v: (v[:, :LANES], v[:, LANES : 2 * LANES], v[:, 2 * LANES :])
    sp_low, sp_high = unpacked(*cut(spectral))
    sp_ref[:rows, :] = sp_low
    sp_ref[rows:, :] = sp_high
    dm_low, dm_high = unpacked(*gathered(gd_ref, 3 * own))
    dm_ref[:rows, :] = dm_low
    dm_ref[rows:, :] = dm_high

    sp_own = jnp.concatenate([sp_low[:own], sp_high[:own]], 0)
    hidden_own = gelu_pair(mul(sp_own, w_in_ref[...]))[0].astype(bf16)
    mask = (sp_own.astype(f32) + mul(hidden_own, w_out_ref[...])).astype(bf16).astype(f32)
    spec = s_ref[...].astype(f32).reshape(2 * own, channels)
    spec_re, spec_im = spec[:, :half_c], spec[:, half_c:]
    mask_re, mask_im = mask[:, :half_c], mask[:, half_c:]
    enhanced = jnp.concatenate(
        [spec_re * mask_re - spec_im * mask_im, spec_re * mask_im + spec_im * mask_re], 1
    )
    enh_ref[...] = enhanced.reshape(frames, bins, channels).astype(bf16)

    gwi_ref[...] = jnp.zeros_like(gwi_ref)
    gwo_ref[...] = jnp.zeros_like(gwo_ref)

    @pl.loop(0, 2 * rows // chunk)
    def _(i):
        at = pl.ds(pl.multiple_of(i * chunk, chunk), chunk)
        sp, dm = sp_ref[at, :], dm_ref[at, :]
        gelu_out, slope = gelu_pair(mul(sp, w_in_ref[...]))
        hidden = gelu_out.astype(bf16)
        dpre = (mul(dm, w_out_ref[...], NT) * slope).astype(bf16)
        gwo_ref[...] += mul(hidden, dm, TN)
        gwi_ref[...] += mul(sp, dpre, TN)
        dsp_ref[at, :] = (dm.astype(f32) + mul(dpre, w_in_ref[...], NT)).astype(bf16)

    dsp_low, dsp_high = dsp_ref[:rows, :], dsp_ref[rows:, :]
    back = mix2[:, :per_block]
    dfirst_low = mul(back, dsp_low, TN).astype(bf16)
    dfirst_high = mul(back, dsp_high, TN).astype(bf16)

    sum_row, sum_col = iota((own, per_block), 0), iota((own, per_block), 1)
    frames_meet = frame_of(sum_row) == frame_of(sum_col)
    to_bin = ((iota((bins, own), 1) & (bins - 1)) == iota((bins, own), 0)).astype(f32)
    col_place = place_of(iota((per_block, block), 0))
    col_want = iota((per_block, block), 1)

    def block_sums(gram, cols):
        return mul_f32(mul_f32(to_bin, jnp.where(frames_meet, gram, 0.0)), cols)

    x_low, x_high = unpacked(*[tile[:own] for tile in x_tiles])
    gram = mul(x_low, dfirst_low, NT) + mul(x_high, dfirst_high, NT)
    g1_ref[...] = block_sums(gram, (col_place == col_want).astype(f32))

    p_row, p_col = iota((own, rows), 0), iota((own, rows), 1)
    chosen = onehot(
        (block_of(p_col) == ((side + (p_row & (bins - 1))) ^ chip))
        & (place_of(p_col) == chip)
        & (frame_of(p_row) == frame_of(p_col))
    )
    first_low, first_high = unpacked(*cut(mul(chosen, first).astype(bf16)))
    gram = mul(first_low, dsp_low[:per_block], NT) + mul(first_high, dsp_high[:per_block], NT)
    g2_ref[...] = block_sums(gram, (col_place == (col_want ^ side)).astype(f32))


def whole_rows(features, spectrum, cotangent, w_first, w_second, w_in, w_out):
    frames, bins, channels = features.shape
    block = w_first.shape[1]
    hid = w_in.shape[1]
    devices = lax.axis_size("freq")
    own = frames // 2 * bins
    vmem = lambda n: [pl.BlockSpec(memory_space=pltpu.VMEM)] * n
    scale = 1.0 / math.sqrt(frames * devices * bins)
    x_own, d_own = pl.pallas_call(
        functools.partial(pack_kernel, scale=scale),
        out_shape=(
            jax.ShapeDtypeStruct((3 * own + W_ROWS, LANES), bf16),
            jax.ShapeDtypeStruct((3 * own, LANES), bf16),
        ),
        in_specs=vmem(5),
        out_specs=tuple(vmem(2)),
        name="pack",
    )(features, spectrum, cotangent, w_first, w_second)

    def gather(value):
        blocks = {0: value}
        for bit in reversed(range(devices.bit_length() - 1)):
            held = jnp.concatenate([blocks[j] for j in sorted(blocks)], 0)
            came = swapped(held, "freq", bit)
            parts = jnp.split(came, len(blocks), 0)
            blocks.update({j ^ 2**bit: part for j, part in zip(sorted(blocks), parts)})
        return jnp.concatenate([blocks[j] for j in range(devices)], 0)

    gx, gd = gather(x_own), gather(d_own)
    rows = devices * own
    return pl.pallas_call(
        functools.partial(main_kernel, chunk=256),
        out_shape=(
            jax.ShapeDtypeStruct((frames, bins, channels), bf16),
            jax.ShapeDtypeStruct((bins, block), f32),
            jax.ShapeDtypeStruct((bins, block), f32),
            jax.ShapeDtypeStruct((channels, hid), f32),
            jax.ShapeDtypeStruct((hid, channels), f32),
        ),
        in_specs=vmem(5),
        out_specs=tuple(vmem(5)),
        scratch_shapes=[pltpu.VMEM((2 * rows, channels), bf16)] * 3,
        compiler_params=pltpu.CompilerParams(vmem_limit_bytes=40 * 2**20),
        name="mix_and_grads",
    )(gx, gd, spectrum, w_in, w_out)


def on_device(features, spectrum, cotangent, w_first, w_second, w_in, w_out):
    frames, bins, channels = features.shape
    block = w_first.shape[1]
    devices = lax.axis_size("freq")
    gathered_bytes = 2 * 2 * devices * frames * bins * channels
    fits = gathered_bytes <= 4 * 2**20
    shaped = (
        block == 2 * bins
        and devices == 2 * block
        and bins <= W_ROWS
        and 2 * block <= LANES
        and LANES < channels
        and 2 * (channels - LANES) == LANES
    )
    plan = whole_rows if fits and shaped else split_rows
    return plan(features, spectrum, cotangent, w_first, w_second, w_in, w_out)


def solution(mesh):
    placed = (
        P("groups", "freq", None),
        P("groups", "freq", None),
        P("groups", "freq", None),
        P("freq", None),
        P("freq", None),
        P(),
        P(),
    )
    return jax.shard_map(
        on_device,
        mesh=mesh,
        in_specs=placed,
        out_specs=(
            P("groups", "freq", None),
            P("freq", "groups"),
            P("freq", "groups"),
            P("groups", None),
            P("groups", None),
        ),
        check_vma=False,
    )
```

```python
import functools
import math

import jax
import jax.numpy as jnp
from jax import lax
from jax.experimental import pallas as pl
from jax.experimental.pallas import tpu as pltpu
from jax.sharding import PartitionSpec as P

gelu_coef = math.sqrt(2.0 / math.pi)


def swapped(value, axis, distance):
    mask = 2**distance
    pairs = [(source, source ^ mask) for source in range(lax.axis_size(axis))]
    return lax.ppermute(value, axis, pairs)


def gelu_pair(pre_act):
    tanh_arg = gelu_coef * (pre_act + 0.044715 * pre_act * pre_act * pre_act)
    tanh_val = jnp.tanh(tanh_arg)
    gelu_out = 0.5 * pre_act * (1.0 + tanh_val)
    gelu_slope = 0.5 * (1.0 + tanh_val) + 0.5 * pre_act * (
        1.0 - tanh_val * tanh_val
    ) * gelu_coef * (1.0 + 3.0 * 0.044715 * pre_act * pre_act)
    return (gelu_out, gelu_slope)


def spread_back(dfirst_two, features):
    frames, own_bins, channels = features.shape
    block = dfirst_two.shape[0]
    quarter = frames // 4
    devices = 2 * block
    send_back = jnp.broadcast_to(dfirst_two[:, None], (block, 2, 2, quarter, channels)).reshape(
        devices, 2 * quarter * channels
    )
    back_rows = lax.all_to_all(send_back, "freq", split_axis=0, concat_axis=0, tiled=True).reshape(
        block, 2, 2, quarter, channels
    )
    by_quarter_x = features.reshape(2, 2, quarter, own_bins, channels)
    return jnp.einsum(
        "hgtbc,pghtc->bp", by_quarter_x, back_rows, preferred_element_type=jnp.float32
    )


def split_rows(features, spectrum, cotangent, w_first, w_second, w_in, w_out):
    frames, own_bins, channels = features.shape
    block = w_first.shape[1]
    quarter = frames // 4
    half_c = channels // 2
    devices = lax.axis_size("freq")
    parity = lax.axis_index("freq") % 2
    lower_side = parity == 0

    def join_halves(mine, theirs, axis):
        return jnp.where(
            lower_side, jnp.concatenate([mine, theirs], axis), jnp.concatenate([theirs, mine], axis)
        )

    got_second = swapped(w_second, "freq", 0)
    full_second = join_halves(w_second, got_second, 0)
    by_quarter = features.reshape(2, 2, quarter, own_bins, channels)
    partials = jnp.einsum(
        "hgtbc,bp->pghtc", by_quarter, w_first, preferred_element_type=jnp.float32
    )
    partials = partials.reshape(devices, 2 * quarter * channels)
    arrived = lax.all_to_all(partials, "freq", split_axis=0, concat_axis=0, tiled=True)
    first_two = arrived.reshape(block, 2, 2, quarter, channels).sum(axis=1).astype(jnp.bfloat16)
    spectral = jnp.einsum(
        "ahtc,aq->htqc", first_two, full_second, preferred_element_type=jnp.float32
    ).astype(jnp.bfloat16)
    flat_rows = spectral.reshape(-1, channels)
    pre_act = jnp.dot(flat_rows, w_in, preferred_element_type=jnp.float32)
    gelu_out, gelu_slope = gelu_pair(pre_act)
    hidden = gelu_out.astype(jnp.bfloat16)
    spectral_mask = (
        flat_rows.astype(jnp.float32) + jnp.dot(hidden, w_out, preferred_element_type=jnp.float32)
    ).astype(jnp.bfloat16)
    spectral_mask = spectral_mask.reshape(2, quarter, block, channels)
    send_mask = lax.dynamic_slice_in_dim(spectral_mask, (1 - parity) * own_bins, own_bins, 2)
    keep_mask = lax.dynamic_slice_in_dim(spectral_mask, parity * own_bins, own_bins, 2)
    got_mask = swapped(send_mask, "freq", 0)
    full_mask = jnp.where(
        lower_side, jnp.stack([keep_mask, got_mask], 1), jnp.stack([got_mask, keep_mask], 1)
    )
    mask_f = full_mask.reshape(frames, own_bins, channels).astype(jnp.float32)
    spec_f = spectrum.astype(jnp.float32)
    mask_re, mask_im = (mask_f[..., :half_c], mask_f[..., half_c:])
    spec_re, spec_im = (spec_f[..., :half_c], spec_f[..., half_c:])
    enhanced = jnp.concatenate(
        [spec_re * mask_re - spec_im * mask_im, spec_re * mask_im + spec_im * mask_re], -1
    ).astype(jnp.bfloat16)
    loss_scale = jnp.float32(1.0) / jnp.sqrt(jnp.float32(frames * devices * own_bins))
    grad_f = cotangent.astype(jnp.float32) * loss_scale
    grad_re, grad_im = (grad_f[..., :half_c], grad_f[..., half_c:])
    dmask = jnp.concatenate(
        [grad_re * spec_re + grad_im * spec_im, grad_im * spec_re - grad_re * spec_im], -1
    ).astype(jnp.bfloat16)
    dmask = dmask.reshape(2, 2, quarter, own_bins, channels)
    send_dmask = lax.dynamic_index_in_dim(dmask, 1 - parity, 1, keepdims=False)
    keep_dmask = lax.dynamic_index_in_dim(dmask, parity, 1, keepdims=False)
    got_dmask = swapped(send_dmask, "freq", 0)
    dmask_rows = join_halves(keep_dmask, got_dmask, 2).reshape(-1, channels)
    dact = jnp.dot(dmask_rows, w_out.T, preferred_element_type=jnp.float32)
    dpre = (dact * gelu_slope).astype(jnp.bfloat16)
    part_out = jnp.dot(hidden.T, dmask_rows, preferred_element_type=jnp.float32)
    part_in = jnp.dot(flat_rows.T, dpre, preferred_element_type=jnp.float32)
    grad_w_in, grad_w_out = lax.psum((part_in, part_out), "freq")
    dspectral = (
        dmask_rows.astype(jnp.float32) + jnp.dot(dpre, w_in.T, preferred_element_type=jnp.float32)
    ).astype(jnp.bfloat16)
    dspectral = dspectral.reshape(2, quarter, block, channels)
    dfirst_two = jnp.einsum(
        "htqc,aq->ahtc", dspectral, full_second, preferred_element_type=jnp.float32
    ).astype(jnp.bfloat16)
    second_part = jnp.einsum(
        "ahtc,htqc->aq", first_two, dspectral, preferred_element_type=jnp.float32
    )
    second_part = second_part.reshape(2, own_bins, block)
    got_part = swapped(
        lax.dynamic_index_in_dim(second_part, 1 - parity, 0, keepdims=False), "freq", 0
    )
    grad_second = lax.dynamic_index_in_dim(second_part, parity, 0, keepdims=False) + got_part
    grad_first = spread_back(dfirst_two, features)
    return (enhanced, grad_first, grad_second, grad_w_in, grad_w_out)


f32, bf16 = jnp.float32, jnp.bfloat16
NN = (((1,), (0,)), ((), ()))
NT = (((1,), (1,)), ((), ()))
TN = (((0,), (0,)), ((), ()))
LANES = 128
W_ROWS = 16
CHUNK = 1024


def mul(a, b, dims=NN):
    return lax.dot_general(a, b, dims, preferred_element_type=f32)


def mul_f32(a, b):
    return lax.dot_general(a, b, NN, precision=lax.Precision.HIGHEST, preferred_element_type=f32)


def iota(shape, dim):
    return lax.broadcasted_iota(jnp.int32, shape, dim)


def onehot(cond):
    return cond.astype(f32).astype(bf16)


def gelu_and_slope(v):
    square = v * v
    tanh_val = jnp.tanh(v * (gelu_coef + (gelu_coef * 0.044715) * square))
    half = 0.5 + 0.5 * tanh_val
    out = v * half
    slope = half + out * (1.0 - half) * (
        2.0 * gelu_coef + (6.0 * gelu_coef * 0.044715) * square
    )
    return out, slope


class Rows:
    def __init__(self, own, bins):
        self.own, self.bins, self.per_block = own, bins, 2 * own
        me = lax.axis_index("freq")
        self.chip, self.side = me >> 1, (me & 1) * bins

    def block(self, r):
        return r // self.per_block

    def place(self, r):
        return ((r // self.own) & 1) * self.bins + (r & (self.bins - 1))

    def frame(self, r):
        return (r // self.bins) & (self.own // self.bins - 1)


def pack_rows(rows):
    half = rows.shape[0] // 2
    low, high = rows[:half], rows[half:]
    rest = jnp.concatenate([low[:, LANES:], high[:, LANES:]], 1)
    return low[:, :LANES], high[:, :LANES], rest


def unpacked(low, high, rest):
    split = rest.shape[1] // 2
    return (
        jnp.concatenate([low, rest[:, :split]], 1),
        jnp.concatenate([high, rest[:, split:]], 1),
    )


def cut(value):
    return value[:, :LANES], value[:, LANES : 2 * LANES], value[:, 2 * LANES :]


def piece(refs, per_device, j, start, size):
    at = (j // 4) * per_device + start
    return refs[j % 4][at : at + size, :]


def tiles_of(refs, per_device, devices, own):
    return [
        jnp.concatenate([piece(refs, per_device, j, t * own, own) for j in range(devices)], 0)
        for t in range(3)
    ]


def pack_kernel(x_ref, s_ref, c_ref, w1_ref, w2_ref, out_ref, spec_ref, *, scale):
    frames, bins, channels = x_ref.shape
    rows = frames * bins
    half = rows // 2
    half_c = channels // 2
    block = w1_ref.shape[1]

    for t, part in enumerate(pack_rows(x_ref[...].astype(f32).reshape(rows, channels))):
        out_ref[t * half : (t + 1) * half, :] = part.astype(bf16)
    weights = jnp.concatenate([w1_ref[...].astype(f32), w2_ref[...].astype(f32)], 1)
    weights = jnp.concatenate([weights, jnp.zeros((bins, LANES - 2 * block), f32)], 1)
    weights = jnp.concatenate([weights, jnp.zeros((W_ROWS - bins, LANES), f32)], 0)
    start = 3 * half + W_ROWS
    out_ref[3 * half : start, :] = weights.astype(bf16)

    spec = s_ref[...].astype(f32).reshape(rows, channels)
    grad = c_ref[...].astype(f32).reshape(rows, channels) * scale
    spec_re, spec_im = spec[:, :half_c], spec[:, half_c:]
    grad_re, grad_im = grad[:, :half_c], grad[:, half_c:]
    dmask = jnp.concatenate(
        [grad_re * spec_re + grad_im * spec_im, grad_im * spec_re - grad_re * spec_im], 1
    )
    for t, part in enumerate(pack_rows(dmask)):
        out_ref[start + t * half : start + (t + 1) * half, :] = part.astype(bf16)
    spec_ref[...] = s_ref[...]


def prepare_kernel(
    own_ref, w_in_hbm, w_out_hbm,
    x_ref, d_ref, w_in_ref, w_out_ref, valid_ref, pick1_ref, spread1_ref, keep1_ref,
    pick2_ref, spread2_ref, keep2_ref, chosen_ref, sems, *, bins,
):
    copies = [
        pltpu.make_async_copy(w_in_hbm, w_in_ref, sems.at[0]),
        pltpu.make_async_copy(w_out_hbm, w_out_ref, sems.at[1]),
    ]
    for copy in copies:
        copy.start()

    x_ref[...] = own_ref[: x_ref.shape[0], :]
    d_ref[...] = own_ref[x_ref.shape[0] :, :]
    own, rows = chosen_ref.shape
    block = 2 * bins
    at = Rows(own, bins)

    def w_place(r):
        return ((r // W_ROWS) & 1) * bins + (r & (W_ROWS - 1))

    def w_block(r):
        return r // (2 * W_ROWS)

    r, w = iota(valid_ref.shape, 0), iota(valid_ref.shape, 1)
    valid_ref[...] = onehot(((w & (W_ROWS - 1)) < bins) & (w_block(w) == at.block(r)))

    r, lane = iota(pick1_ref.shape, 0), iota(pick1_ref.shape, 1)
    pick1_ref[...] = onehot(lane == at.place(r))
    pick2_ref[...] = onehot(lane == block + (at.place(r) ^ at.side))

    w, r = iota(spread1_ref.shape, 0), iota(spread1_ref.shape, 1)
    spread1_ref[...] = onehot((w_place(w) == at.place(r)) & (w_block(w) == at.block(r)))
    spread2_ref[...] = onehot(w_place(w) == (at.block(r) ^ at.chip ^ at.side))

    row, col = iota(keep1_ref.shape, 0), iota(keep1_ref.shape, 1)
    same_frame = at.frame(row) == at.frame(col)
    keep1_ref[...] = onehot(same_frame)
    keep2_ref[...] = onehot(same_frame & (at.place(col) == (at.block(row) ^ at.chip)))

    row, col = iota(chosen_ref.shape, 0), iota(chosen_ref.shape, 1)
    chosen_ref[...] = onehot(
        (at.block(col) == ((at.side + (row & (bins - 1))) ^ at.chip))
        & (at.place(col) == at.chip)
        & (at.frame(row) == at.frame(col))
    )
    for copy in copies:
        copy.wait()


def forward_kernel(
    x0, x1, x2, x3, w_in_ref, valid_ref, pick1_ref, spread1_ref, keep1_ref,
    pick2_ref, spread2_ref, keep2_ref, chosen_ref,
    hid_ref, slope_ref, spt_ref, back_ref, first_ref, own_ref, sp_own_ref,
    sp_ref,
):
    own = own_ref.shape[0] // 2
    per_x = 3 * own + W_ROWS
    devices = 4 * x0.shape[0] // per_x
    rows = devices * own
    refs = (x0, x1, x2, x3)

    x_tiles = tiles_of(refs, per_x, devices, own)
    weights = jnp.concatenate(
        [piece(refs, per_x, j, 3 * own, W_ROWS) for j in range(devices)], 0
    )

    def mixing(pick, spread, keep):
        of_row = mul(pick[...], weights, NT).astype(bf16) * valid_ref[...]
        return mul(of_row, spread[...]).astype(bf16) * keep[...]

    mix1 = mixing(pick1_ref, spread1_ref, keep1_ref)
    mix2 = mixing(pick2_ref, spread2_ref, keep2_ref)
    back_ref[...] = mix2[:, : 2 * own]

    first = mul(mix1, jnp.concatenate(x_tiles, 1)).astype(bf16)
    spectral = mul(mix2, first).astype(bf16)
    sp_low, sp_high = unpacked(*cut(spectral))
    sp_ref[:rows, :] = sp_low
    sp_ref[rows:, :] = sp_high
    sp_own_ref[:own, :], sp_own_ref[own:, :] = sp_low[:own], sp_high[:own]
    own_ref[:own, :], own_ref[own:, :] = unpacked(*[tile[:own] for tile in x_tiles])

    first_ref[:own, :], first_ref[own:, :] = unpacked(
        *cut(mul(chosen_ref[...], first).astype(bf16))
    )

    @pl.loop(0, 2 * rows // CHUNK)
    def _(i):
        here = pl.ds(pl.multiple_of(i * CHUNK, CHUNK), CHUNK)
        sp = sp_ref[here, :]
        gelu_out, slope = gelu_and_slope(mul(sp, w_in_ref[...]))
        hid_ref[here, :] = gelu_out.astype(bf16)
        slope_ref[here, :] = slope
        spt_ref[:, here] = sp.T


def backward_kernel(
    d0, d1, d2, d3, hid_ref, slope_ref, spt_ref, back_ref, first_ref, own_ref, sp_own_ref,
    s_ref, w_in_ref, w_out_ref,
    enh_ref, g1_ref, g2_ref, gwi_ref, gwo_ref,
    dm_ref, dsp_ref,
):
    bins, block = g1_ref.shape
    frames, _, channels = s_ref.shape
    half_c = channels // 2
    own = own_ref.shape[0] // 2
    devices = 4 * d0.shape[0] // (3 * own)
    rows = devices * own
    at = Rows(own, bins)
    dm_low, dm_high = unpacked(*tiles_of((d0, d1, d2, d3), 3 * own, devices, own))
    dm_ref[:rows, :] = dm_low
    dm_ref[rows:, :] = dm_high

    sp_own = sp_own_ref[...]
    hidden = jnp.concatenate([hid_ref[:own, :], hid_ref[rows : rows + own, :]], 0)
    mask = (sp_own.astype(f32) + mul(hidden, w_out_ref[...], NT)).astype(bf16).astype(f32)
    spec = s_ref[...].astype(f32).reshape(2 * own, channels)
    spec_re, spec_im = spec[:, :half_c], spec[:, half_c:]
    mask_re, mask_im = mask[:, :half_c], mask[:, half_c:]
    enhanced = jnp.concatenate(
        [spec_re * mask_re - spec_im * mask_im, spec_re * mask_im + spec_im * mask_re], 1
    )
    enh_ref[...] = enhanced.reshape(frames, bins, channels).astype(bf16)

    gwi_ref[...] = jnp.zeros_like(gwi_ref)
    gwo_ref[...] = jnp.zeros_like(gwo_ref)

    @pl.loop(0, 2 * rows // CHUNK)
    def _(i):
        here = pl.ds(pl.multiple_of(i * CHUNK, CHUNK), CHUNK)
        dm = dm_ref[here, :]
        dpre = (mul(dm, w_out_ref[...]) * slope_ref[here, :]).astype(bf16)
        gwo_ref[...] += mul(dm, hid_ref[here, :], TN)
        gwi_ref[...] += mul(spt_ref[:, here], dpre)
        dsp_ref[here, :] = (dm.astype(f32) + mul(dpre, w_in_ref[...], NT)).astype(bf16)

    dsp_low, dsp_high = dsp_ref[:rows, :], dsp_ref[rows:, :]
    dfirst_low = mul(back_ref[...], dsp_low, TN).astype(bf16)
    dfirst_high = mul(back_ref[...], dsp_high, TN).astype(bf16)

    per_block = at.per_block
    frames_meet = at.frame(iota((own, per_block), 0)) == at.frame(iota((own, per_block), 1))

    def bin_sums(gram):
        parts = jnp.where(frames_meet, gram, 0.0)
        total = sum(parts[n : n + 2 * bins] for n in range(0, own, 2 * bins))
        return total[:bins] + total[bins:]

    gram = mul(own_ref[:own, :], dfirst_low, NT) + mul(own_ref[own:, :], dfirst_high, NT)
    sums = [bin_sums(gram)]
    gram = mul(first_ref[:own, :], dsp_low[:per_block], NT)
    gram += mul(first_ref[own:, :], dsp_high[:per_block], NT)
    sums.append(bin_sums(gram))
    row, col = iota((2 * per_block, 2 * block), 0), iota((2 * per_block, 2 * block), 1)
    place = at.place(row & (per_block - 1))
    take = ((row < per_block) & (place == col)) | (
        (row >= per_block) & (block + (place ^ at.side) == col)
    )
    both = mul_f32(jnp.concatenate(sums, 1), take.astype(f32))
    g1_ref[...] = both[:, :block]
    g2_ref[...] = both[:, block:]


def whole_rows(features, spectrum, cotangent, w_first, w_second, w_in, w_out):
    frames, bins, channels = features.shape
    block = w_first.shape[1]
    hid = w_in.shape[1]
    devices = lax.axis_size("freq")
    own = frames // 2 * bins
    rows = devices * own
    in_vmem = lambda n: [pl.BlockSpec(memory_space=pltpu.VMEM)] * n
    in_hbm = lambda n: [pl.BlockSpec(memory_space=pltpu.HBM)] * n
    shaped = jax.ShapeDtypeStruct
    params = pltpu.CompilerParams(vmem_limit_bytes=40 * 2**20)
    scale = 1.0 / math.sqrt(frames * devices * bins)
    own_rows, spec_in = pl.pallas_call(
        functools.partial(pack_kernel, scale=scale),
        out_shape=(
            pltpu.VMEM((6 * own + W_ROWS, LANES), bf16),
            pltpu.VMEM((frames, bins, channels), bf16),
        ),
        in_specs=in_vmem(5),
        out_specs=tuple(in_vmem(2)),
        name="pack",
    )(features, spectrum, cotangent, w_first, w_second)
    w_rows = devices * W_ROWS
    x_own, d_own, w_in_in, w_out_in, *selections = pl.pallas_call(
        functools.partial(prepare_kernel, bins=bins),
        out_shape=tuple(
            pltpu.VMEM(shape, bf16)
            for shape in [
                (3 * own + W_ROWS, LANES),
                (3 * own, LANES),
                (channels, hid),
                (channels, hid),
                (rows, w_rows),
                (rows, LANES),
                (w_rows, rows),
                (rows, rows),
                (rows, LANES),
                (w_rows, rows),
                (rows, rows),
                (own, rows),
            ]
        ),
        in_specs=in_vmem(1) + in_hbm(2),
        out_specs=tuple(in_vmem(12)),
        scratch_shapes=[pltpu.SemaphoreType.DMA((2,))],
        compiler_params=params,
        cost_estimate=pl.CostEstimate(flops=0, bytes_accessed=2**21, transcendentals=0),
        name="prepare",
    )(own_rows, w_in, w_out.T)

    columns = [exchanged(own_rows, j) for j in range(devices - 4, 0, -4)][::-1]
    x_rows = 3 * own + W_ROWS
    x0 = jnp.concatenate([x_own] + [column[:x_rows] for column in columns], 0)
    d0 = jnp.concatenate([d_own] + [column[x_rows:] for column in columns], 0)
    x2, d2 = exchanged(x0, 2), exchanged(d0, 2)
    x1, d1 = exchanged(x0, 1), exchanged(d0, 1)
    x3, d3 = exchanged(x2, 1), exchanged(d2, 1)

    kept = pl.pallas_call(
        forward_kernel,
        out_shape=(
            shaped((2 * rows, hid), bf16),
            shaped((2 * rows, hid), f32),
            shaped((channels, 2 * rows), bf16),
            shaped((rows, 2 * own), bf16),
            shaped((2 * own, channels), bf16),
            shaped((2 * own, channels), bf16),
            shaped((2 * own, channels), bf16),
        ),
        in_specs=in_vmem(13),
        out_specs=tuple(in_vmem(7)),
        scratch_shapes=[pltpu.VMEM((2 * rows, channels), bf16)],
        compiler_params=params,
        name="forward",
    )(x0, x1, x2, x3, w_in_in, *selections)

    enhanced, grad_first, grad_second, grad_w_in, grad_w_out = pl.pallas_call(
        backward_kernel,
        out_shape=(
            shaped((frames, bins, channels), bf16),
            shaped((bins, block), f32),
            shaped((bins, block), f32),
            shaped((channels, hid), f32),
            shaped((channels, hid), f32),
        ),
        in_specs=in_vmem(14),
        out_specs=tuple(in_vmem(5)),
        scratch_shapes=[pltpu.VMEM((2 * rows, channels), bf16)] * 2,
        compiler_params=params,
        name="backward",
    )(d0, d1, d2, d3, *kept, spec_in, w_in_in, w_out_in)
    return enhanced, grad_first, grad_second, grad_w_in, grad_w_out.T


def exchanged(value, mask):
    pairs = [(source, source ^ mask) for source in range(lax.axis_size("freq"))]
    return lax.ppermute(value, "freq", pairs)


def on_device(features, spectrum, cotangent, w_first, w_second, w_in, w_out):
    frames, bins, channels = features.shape
    block = w_first.shape[1]
    devices = lax.axis_size("freq")
    gathered_bytes = 2 * 2 * devices * frames * bins * channels
    fits = gathered_bytes <= 4 * 2**20
    shaped = (
        block == 2 * bins
        and devices == 2 * block
        and bins <= W_ROWS
        and 2 * block <= LANES
        and LANES < channels
        and 2 * (channels - LANES) == LANES
        and devices % 4 == 0
    )
    plan = whole_rows if fits and shaped else split_rows
    return plan(features, spectrum, cotangent, w_first, w_second, w_in, w_out)


def solution(mesh):
    placed = (
        P("groups", "freq", None),
        P("groups", "freq", None),
        P("groups", "freq", None),
        P("freq", None),
        P("freq", None),
        P(),
        P(),
    )
    return jax.shard_map(
        on_device,
        mesh=mesh,
        in_specs=placed,
        out_specs=(
            P("groups", "freq", None),
            P("freq", "groups"),
            P("freq", "groups"),
            P("groups", None),
            P("groups", None),
        ),
        check_vma=False,
    )
```

```python
import functools
import math

import jax
import jax.numpy as jnp
from jax import lax
from jax.experimental import pallas as pl
from jax.experimental.pallas import tpu as pltpu
from jax.sharding import PartitionSpec as P

gelu_coef = math.sqrt(2.0 / math.pi)


def swapped(value, axis, distance):
    mask = 2**distance
    pairs = [(source, source ^ mask) for source in range(lax.axis_size(axis))]
    return lax.ppermute(value, axis, pairs)


def gelu_pair(pre_act):
    tanh_arg = gelu_coef * (pre_act + 0.044715 * pre_act * pre_act * pre_act)
    tanh_val = jnp.tanh(tanh_arg)
    gelu_out = 0.5 * pre_act * (1.0 + tanh_val)
    gelu_slope = 0.5 * (1.0 + tanh_val) + 0.5 * pre_act * (
        1.0 - tanh_val * tanh_val
    ) * gelu_coef * (1.0 + 3.0 * 0.044715 * pre_act * pre_act)
    return (gelu_out, gelu_slope)


def spread_back(dfirst_two, features):
    frames, own_bins, channels = features.shape
    block = dfirst_two.shape[0]
    quarter = frames // 4
    devices = 2 * block
    send_back = jnp.broadcast_to(dfirst_two[:, None], (block, 2, 2, quarter, channels)).reshape(
        devices, 2 * quarter * channels
    )
    back_rows = lax.all_to_all(send_back, "freq", split_axis=0, concat_axis=0, tiled=True).reshape(
        block, 2, 2, quarter, channels
    )
    by_quarter_x = features.reshape(2, 2, quarter, own_bins, channels)
    return jnp.einsum(
        "hgtbc,pghtc->bp", by_quarter_x, back_rows, preferred_element_type=jnp.float32
    )


def split_rows(features, spectrum, cotangent, w_first, w_second, w_in, w_out):
    frames, own_bins, channels = features.shape
    block = w_first.shape[1]
    quarter = frames // 4
    half_c = channels // 2
    devices = lax.axis_size("freq")
    parity = lax.axis_index("freq") % 2
    lower_side = parity == 0

    def join_halves(mine, theirs, axis):
        return jnp.where(
            lower_side, jnp.concatenate([mine, theirs], axis), jnp.concatenate([theirs, mine], axis)
        )

    got_second = swapped(w_second, "freq", 0)
    full_second = join_halves(w_second, got_second, 0)
    by_quarter = features.reshape(2, 2, quarter, own_bins, channels)
    partials = jnp.einsum(
        "hgtbc,bp->pghtc", by_quarter, w_first, preferred_element_type=jnp.float32
    )
    partials = partials.reshape(devices, 2 * quarter * channels)
    arrived = lax.all_to_all(partials, "freq", split_axis=0, concat_axis=0, tiled=True)
    first_two = arrived.reshape(block, 2, 2, quarter, channels).sum(axis=1).astype(jnp.bfloat16)
    spectral = jnp.einsum(
        "ahtc,aq->htqc", first_two, full_second, preferred_element_type=jnp.float32
    ).astype(jnp.bfloat16)
    flat_rows = spectral.reshape(-1, channels)
    pre_act = jnp.dot(flat_rows, w_in, preferred_element_type=jnp.float32)
    gelu_out, gelu_slope = gelu_pair(pre_act)
    hidden = gelu_out.astype(jnp.bfloat16)
    spectral_mask = (
        flat_rows.astype(jnp.float32) + jnp.dot(hidden, w_out, preferred_element_type=jnp.float32)
    ).astype(jnp.bfloat16)
    spectral_mask = spectral_mask.reshape(2, quarter, block, channels)
    send_mask = lax.dynamic_slice_in_dim(spectral_mask, (1 - parity) * own_bins, own_bins, 2)
    keep_mask = lax.dynamic_slice_in_dim(spectral_mask, parity * own_bins, own_bins, 2)
    got_mask = swapped(send_mask, "freq", 0)
    full_mask = jnp.where(
        lower_side, jnp.stack([keep_mask, got_mask], 1), jnp.stack([got_mask, keep_mask], 1)
    )
    mask_f = full_mask.reshape(frames, own_bins, channels).astype(jnp.float32)
    spec_f = spectrum.astype(jnp.float32)
    mask_re, mask_im = (mask_f[..., :half_c], mask_f[..., half_c:])
    spec_re, spec_im = (spec_f[..., :half_c], spec_f[..., half_c:])
    enhanced = jnp.concatenate(
        [spec_re * mask_re - spec_im * mask_im, spec_re * mask_im + spec_im * mask_re], -1
    ).astype(jnp.bfloat16)
    loss_scale = jnp.float32(1.0) / jnp.sqrt(jnp.float32(frames * devices * own_bins))
    grad_f = cotangent.astype(jnp.float32) * loss_scale
    grad_re, grad_im = (grad_f[..., :half_c], grad_f[..., half_c:])
    dmask = jnp.concatenate(
        [grad_re * spec_re + grad_im * spec_im, grad_im * spec_re - grad_re * spec_im], -1
    ).astype(jnp.bfloat16)
    dmask = dmask.reshape(2, 2, quarter, own_bins, channels)
    send_dmask = lax.dynamic_index_in_dim(dmask, 1 - parity, 1, keepdims=False)
    keep_dmask = lax.dynamic_index_in_dim(dmask, parity, 1, keepdims=False)
    got_dmask = swapped(send_dmask, "freq", 0)
    dmask_rows = join_halves(keep_dmask, got_dmask, 2).reshape(-1, channels)
    dact = jnp.dot(dmask_rows, w_out.T, preferred_element_type=jnp.float32)
    dpre = (dact * gelu_slope).astype(jnp.bfloat16)
    part_out = jnp.dot(hidden.T, dmask_rows, preferred_element_type=jnp.float32)
    part_in = jnp.dot(flat_rows.T, dpre, preferred_element_type=jnp.float32)
    grad_w_in, grad_w_out = lax.psum((part_in, part_out), "freq")
    dspectral = (
        dmask_rows.astype(jnp.float32) + jnp.dot(dpre, w_in.T, preferred_element_type=jnp.float32)
    ).astype(jnp.bfloat16)
    dspectral = dspectral.reshape(2, quarter, block, channels)
    dfirst_two = jnp.einsum(
        "htqc,aq->ahtc", dspectral, full_second, preferred_element_type=jnp.float32
    ).astype(jnp.bfloat16)
    second_part = jnp.einsum(
        "ahtc,htqc->aq", first_two, dspectral, preferred_element_type=jnp.float32
    )
    second_part = second_part.reshape(2, own_bins, block)
    got_part = swapped(
        lax.dynamic_index_in_dim(second_part, 1 - parity, 0, keepdims=False), "freq", 0
    )
    grad_second = lax.dynamic_index_in_dim(second_part, parity, 0, keepdims=False) + got_part
    grad_first = spread_back(dfirst_two, features)
    return (enhanced, grad_first, grad_second, grad_w_in, grad_w_out)


f32, bf16 = jnp.float32, jnp.bfloat16
NN = (((1,), (0,)), ((), ()))
NT = (((1,), (1,)), ((), ()))
TN = (((0,), (0,)), ((), ()))
LANES = 128
W_ROWS = 16


def mul(a, b, dims=NN):
    return lax.dot_general(a, b, dims, preferred_element_type=f32)


def mul_f32(a, b):
    return lax.dot_general(a, b, NN, precision=lax.Precision.HIGHEST, preferred_element_type=f32)


def iota(shape, dim):
    return lax.broadcasted_iota(jnp.int32, shape, dim)


def onehot(cond):
    return cond.astype(f32).astype(bf16)


def gelu_and_slope(v):
    square = v * v
    tanh_val = jnp.tanh(v * (gelu_coef + (gelu_coef * 0.044715) * square))
    half = 0.5 + 0.5 * tanh_val
    out = v * half
    slope = half + out * (1.0 - half) * (
        2.0 * gelu_coef + (6.0 * gelu_coef * 0.044715) * square
    )
    return out, slope


class Rows:
    def __init__(self, own, bins):
        self.own, self.bins, self.per_block = own, bins, 2 * own
        me = lax.axis_index("freq")
        self.chip, self.side = me >> 1, (me & 1) * bins

    def block(self, r):
        return r // self.per_block

    def place(self, r):
        return ((r // self.own) & 1) * self.bins + (r & (self.bins - 1))

    def frame(self, r):
        return (r // self.bins) & (self.own // self.bins - 1)


def pack_rows(rows):
    half = rows.shape[0] // 2
    low, high = rows[:half], rows[half:]
    rest = jnp.concatenate([low[:, LANES:], high[:, LANES:]], 1)
    return low[:, :LANES], high[:, :LANES], rest


def unpacked(low, high, rest):
    split = rest.shape[1] // 2
    return (
        jnp.concatenate([low, rest[:, :split]], 1),
        jnp.concatenate([high, rest[:, split:]], 1),
    )


def cut(value):
    return value[:, :LANES], value[:, LANES : 2 * LANES], value[:, 2 * LANES :]


def received_from(devices):
    column = [*range(devices - 4, 0, -4)]
    near, far = [*column, 0], [j ^ 2 for j in [*column, 0]]
    return [near, [j ^ 1 for j in near], far, [j ^ 1 for j in far]]


def piece(refs, per_device, j, start, size):
    held = received_from(sum(ref.shape[0] for ref in refs) // per_device)
    n = next(n for n, part in enumerate(held) if j in part)
    at = held[n].index(j) * per_device + start
    return refs[n][at : at + size, :]


def tiles_of(refs, per_device, devices, own):
    return [
        jnp.concatenate([piece(refs, per_device, j, t * own, own) for j in range(devices)], 0)
        for t in range(3)
    ]


def pack_kernel(
    x_hbm, s_hbm, c_hbm, w1_hbm, w2_hbm, w_in_hbm, w_out_hbm,
    out_ref, s_ref, w_in_ref, w_out_ref,
    x_ref, c_ref, w1_ref, w2_ref, sems, *, scale,
):
    copies = [
        pltpu.make_async_copy(src, dst, sems.at[n])
        for n, (src, dst) in enumerate(
            [
                (x_hbm, x_ref),
                (w1_hbm, w1_ref),
                (w2_hbm, w2_ref),
                (s_hbm, s_ref),
                (c_hbm, c_ref),
                (w_in_hbm, w_in_ref),
                (w_out_hbm, w_out_ref),
            ]
        )
    ]
    for copy in copies:
        copy.start()
    for copy in copies[:3]:
        copy.wait()
    frames, bins, channels = x_ref.shape
    rows = frames * bins
    half = rows // 2
    half_c = channels // 2
    block = w1_ref.shape[1]

    for t, part in enumerate(pack_rows(x_ref[...].astype(f32).reshape(rows, channels))):
        out_ref[t * half : (t + 1) * half, :] = part.astype(bf16)
    weights = jnp.concatenate([w1_ref[...].astype(f32), w2_ref[...].astype(f32)], 1)
    weights = jnp.concatenate([weights, jnp.zeros((bins, LANES - 2 * block), f32)], 1)
    weights = jnp.concatenate([weights, jnp.zeros((W_ROWS - bins, LANES), f32)], 0)
    start = 3 * half + W_ROWS
    out_ref[3 * half : start, :] = weights.astype(bf16)

    for copy in copies[3:5]:
        copy.wait()
    spec = s_ref[...].astype(f32).reshape(rows, channels)
    grad = c_ref[...].astype(f32).reshape(rows, channels) * scale
    spec_re, spec_im = spec[:, :half_c], spec[:, half_c:]
    grad_re, grad_im = grad[:, :half_c], grad[:, half_c:]
    dmask = jnp.concatenate(
        [grad_re * spec_re + grad_im * spec_im, grad_im * spec_re - grad_re * spec_im], 1
    )
    for t, part in enumerate(pack_rows(dmask)):
        out_ref[start + t * half : start + (t + 1) * half, :] = part.astype(bf16)
    for copy in copies[5:]:
        copy.wait()


def prepare_kernel(
    own_ref, w_in_ref, x_ref, d_ref, w_in_t_ref, valid_ref, pick1_ref, spread1_ref, keep1_ref,
    pick2_ref, spread2_ref, keep2_ref, chosen_ref, *, bins,
):
    w_in_t_ref[...] = w_in_ref[...].T
    x_ref[...] = own_ref[: x_ref.shape[0], :]
    d_ref[...] = own_ref[x_ref.shape[0] :, :]
    own, rows = chosen_ref.shape
    block = 2 * bins
    at = Rows(own, bins)

    def w_place(r):
        return ((r // W_ROWS) & 1) * bins + (r & (W_ROWS - 1))

    def w_block(r):
        return r // (2 * W_ROWS)

    r, w = iota(valid_ref.shape, 0), iota(valid_ref.shape, 1)
    valid_ref[...] = onehot(((w & (W_ROWS - 1)) < bins) & (w_block(w) == at.block(r)))

    r, lane = iota(pick1_ref.shape, 0), iota(pick1_ref.shape, 1)
    pick1_ref[...] = onehot(lane == at.place(r))
    pick2_ref[...] = onehot(lane == block + (at.place(r) ^ at.side))

    w, r = iota(spread1_ref.shape, 0), iota(spread1_ref.shape, 1)
    spread1_ref[...] = onehot((w_place(w) == at.place(r)) & (w_block(w) == at.block(r)))
    w, r = iota(spread2_ref.shape, 0), iota(spread2_ref.shape, 1)
    spread2_ref[...] = onehot(w_place(w) == (at.block(r) ^ at.chip ^ at.side))

    row, col = iota(keep1_ref.shape, 0), iota(keep1_ref.shape, 1)
    keep1_ref[...] = onehot(at.frame(row) == at.frame(col))
    row, col = iota(keep2_ref.shape, 0), iota(keep2_ref.shape, 1)
    keep2_ref[...] = onehot(
        (at.frame(row) == at.frame(col)) & (at.place(col) == (at.block(row) ^ at.chip))
    )

    row, col = iota(chosen_ref.shape, 0), iota(chosen_ref.shape, 1)
    chosen_ref[...] = onehot(
        (at.block(col) == ((at.side + (row & (bins - 1))) ^ at.chip))
        & (at.place(col) == at.chip)
        & (at.frame(row) == at.frame(col))
    )


def forward_kernel(
    x0, x1, x2, x3, w_in_ref, valid_ref, pick1_ref, spread1_ref, keep1_ref,
    pick2_ref, spread2_ref, keep2_ref, chosen_ref,
    hid_ref, slope_ref, spt_ref, back_ref, first_ref, own_ref, sp_own_ref,
):
    own = own_ref.shape[0] // 2
    per_x = 3 * own + W_ROWS
    refs = (x0, x1, x2, x3)
    devices = sum(ref.shape[0] for ref in refs) // per_x
    rows = devices * own

    x_tiles = tiles_of(refs, per_x, devices, own)
    weights = jnp.concatenate(
        [piece(refs, per_x, j, 3 * own, W_ROWS) for j in range(devices)], 0
    )

    packed_x = jnp.concatenate(x_tiles, 1)
    half_rows, half_w = rows // 2, weights.shape[0] // 2
    halves = [slice(0, half_rows), slice(half_rows, rows)]
    factors = [weights[:half_w], weights[half_w:]]
    picked = [
        [mul(pick[...], f, NT).astype(bf16) * valid_ref[...] for f in factors]
        for pick in (pick1_ref, pick2_ref)
    ]
    mix1 = [mul(p, spread1_ref[...]).astype(bf16) * keep1_ref[...] for p in picked[0]]
    mix2 = [
        mul(p, spread2_ref[...]).astype(bf16) * keep2_ref[here, :]
        for p, here in zip(picked[1], halves)
    ]
    first = jnp.concatenate([mul(m, packed_x[here]).astype(bf16) for m, here in zip(mix1, halves)], 0)
    spectral = jnp.concatenate([mul(m, first).astype(bf16) for m in mix2], 0)
    for m, here in zip(mix2, halves):
        back_ref[here, :] = m[:, : 2 * own]
    sp_low, sp_high = unpacked(*cut(spectral))
    sp_own_ref[:own, :], sp_own_ref[own:, :] = sp_low[:own], sp_high[:own]
    own_ref[:own, :], own_ref[own:, :] = unpacked(*[tile[:own] for tile in x_tiles])

    first_ref[:own, :], first_ref[own:, :] = unpacked(
        *cut(mul(chosen_ref[...], first).astype(bf16))
    )

    sp = jnp.concatenate([sp_low, sp_high], 0)
    gelu_out, slope = gelu_and_slope(mul(sp, w_in_ref[...]))
    hid_ref[...] = gelu_out.astype(bf16)
    slope_ref[...] = slope
    spt_ref[...] = sp.T


def backward_kernel(
    d0, d1, d2, d3, hid_ref, slope_ref, spt_ref, back_ref, first_ref, own_ref, sp_own_ref,
    s_ref, w_in_t_ref, w_out_ref,
    enh_ref, g1_ref, g2_ref, gwi_ref, gwo_ref,
):
    bins, block = g1_ref.shape
    frames, _, channels = s_ref.shape
    half_c = channels // 2
    own = own_ref.shape[0] // 2
    refs = (d0, d1, d2, d3)
    devices = sum(ref.shape[0] for ref in refs) // (3 * own)
    rows = devices * own
    at = Rows(own, bins)
    dm_low, dm_high = unpacked(*tiles_of(refs, 3 * own, devices, own))
    dpre, dsp = [], []
    for n, part in enumerate((dm_low, dm_high)):
        to = slice(n * rows, (n + 1) * rows)
        dpre.append((mul(part, w_out_ref[...]) * slope_ref[to, :]).astype(bf16))
    for n, part in enumerate((dm_low, dm_high)):
        dsp.append((part.astype(f32) + mul(dpre[n], w_in_t_ref[...])).astype(bf16))
    gwi_ref[...] = mul(spt_ref[:, :rows], dpre[0]) + mul(spt_ref[:, rows:], dpre[1])
    gwo_ref[...] = mul(dm_low, hid_ref[:rows, :], TN) + mul(dm_high, hid_ref[rows:, :], TN)

    sp_own = sp_own_ref[...]
    hidden = jnp.concatenate([hid_ref[:own, :], hid_ref[rows : rows + own, :]], 0)
    mask = (sp_own.astype(f32) + mul(hidden, w_out_ref[...], NT)).astype(bf16).astype(f32)
    spec = s_ref[...].astype(f32).reshape(2 * own, channels)
    spec_re, spec_im = spec[:, :half_c], spec[:, half_c:]
    mask_re, mask_im = mask[:, :half_c], mask[:, half_c:]
    enhanced = jnp.concatenate(
        [spec_re * mask_re - spec_im * mask_im, spec_re * mask_im + spec_im * mask_re], 1
    )
    enh_ref[...] = enhanced.reshape(frames, bins, channels).astype(bf16)

    dsp_low, dsp_high = dsp
    dfirst_low = mul(back_ref[...], dsp_low, TN).astype(bf16)
    dfirst_high = mul(back_ref[...], dsp_high, TN).astype(bf16)

    per_block = at.per_block
    frames_meet = at.frame(iota((own, per_block), 0)) == at.frame(iota((own, per_block), 1))

    def bin_sums(gram):
        parts = jnp.where(frames_meet, gram, 0.0)
        total = sum(parts[n : n + 2 * bins] for n in range(0, own, 2 * bins))
        return total[:bins] + total[bins:]

    gram = mul(own_ref[:own, :], dfirst_low, NT) + mul(own_ref[own:, :], dfirst_high, NT)
    sums = [bin_sums(gram)]
    gram = mul(first_ref[:own, :], dsp_low[:per_block], NT)
    gram += mul(first_ref[own:, :], dsp_high[:per_block], NT)
    sums.append(bin_sums(gram))
    row, col = iota((2 * per_block, 2 * block), 0), iota((2 * per_block, 2 * block), 1)
    place = at.place(row & (per_block - 1))
    take = ((row < per_block) & (place == col)) | (
        (row >= per_block) & (block + (place ^ at.side) == col)
    )
    both = mul_f32(jnp.concatenate(sums, 1), take.astype(f32))
    g1_ref[...] = both[:, :block]
    g2_ref[...] = both[:, block:]


def whole_rows(features, spectrum, cotangent, w_first, w_second, w_in, w_out):
    frames, bins, channels = features.shape
    block = w_first.shape[1]
    hid = w_in.shape[1]
    devices = lax.axis_size("freq")
    own = frames // 2 * bins
    rows = devices * own
    in_vmem = lambda n: [pl.BlockSpec(memory_space=pltpu.VMEM)] * n
    in_hbm = lambda n: [pl.BlockSpec(memory_space=pltpu.HBM)] * n
    shaped = jax.ShapeDtypeStruct
    params = pltpu.CompilerParams(vmem_limit_bytes=40 * 2**20)
    scale = 1.0 / math.sqrt(frames * devices * bins)
    own_rows, spec_in, w_in_in, w_out_in = pl.pallas_call(
        functools.partial(pack_kernel, scale=scale),
        out_shape=(
            pltpu.VMEM((6 * own + W_ROWS, LANES), bf16),
            pltpu.VMEM((frames, bins, channels), bf16),
            pltpu.VMEM((channels, hid), bf16),
            pltpu.VMEM((channels, hid), bf16),
        ),
        in_specs=in_hbm(7),
        out_specs=tuple(in_vmem(4)),
        scratch_shapes=[
            pltpu.VMEM((frames, bins, channels), bf16),
            pltpu.VMEM((frames, bins, channels), bf16),
            pltpu.VMEM((bins, block), bf16),
            pltpu.VMEM((bins, block), bf16),
            pltpu.SemaphoreType.DMA((7,)),
        ],
        name="pack",
    )(features, spectrum, cotangent, w_first, w_second, w_in, w_out.T)
    w_rows = devices * W_ROWS
    x_own, d_own, w_in_t, *selections = pl.pallas_call(
        functools.partial(prepare_kernel, bins=bins),
        out_shape=tuple(
            pltpu.VMEM(shape, bf16)
            for shape in [
                (3 * own + W_ROWS, LANES),
                (3 * own, LANES),
                (hid, channels),
                (rows // 2, w_rows // 2),
                (rows // 2, LANES),
                (w_rows // 2, rows // 2),
                (rows // 2, rows // 2),
                (rows // 2, LANES),
                (w_rows // 2, rows),
                (rows, rows),
                (own, rows),
            ]
        ),
        in_specs=in_vmem(2),
        out_specs=tuple(in_vmem(11)),
        compiler_params=params,
        cost_estimate=pl.CostEstimate(flops=0, bytes_accessed=2**21, transcendentals=0),
        name="prepare",
    )(own_rows, w_in_in)

    column = [exchanged(own_rows, j) for j in range(devices - 4, 0, -4)]
    x_rows = 3 * own + W_ROWS
    x_column = jnp.concatenate([*[got[:x_rows] for got in column], x_own], 0)
    d_column = jnp.concatenate([*[got[x_rows:] for got in column], d_own], 0)
    x2, d2 = exchanged(x_column, 2), exchanged(d_column, 2)
    x0 = x_column
    d0 = d_column
    x1, d1 = exchanged(x0, 1), exchanged(d0, 1)
    x3, d3 = exchanged(x2, 1), exchanged(d2, 1)

    kept = pl.pallas_call(
        forward_kernel,
        out_shape=(
            shaped((2 * rows, hid), bf16),
            shaped((2 * rows, hid), f32),
            shaped((channels, 2 * rows), bf16),
            shaped((rows, 2 * own), bf16),
            shaped((2 * own, channels), bf16),
            shaped((2 * own, channels), bf16),
            shaped((2 * own, channels), bf16),
        ),
        in_specs=in_vmem(13),
        out_specs=tuple(in_vmem(7)),
        compiler_params=params,
        name="forward",
    )(x0, x1, x2, x3, w_in_in, *selections)

    enhanced, grad_first, grad_second, grad_w_in, grad_w_out = pl.pallas_call(
        backward_kernel,
        out_shape=(
            shaped((frames, bins, channels), bf16),
            shaped((bins, block), f32),
            shaped((bins, block), f32),
            shaped((channels, hid), f32),
            shaped((channels, hid), f32),
        ),
        in_specs=in_vmem(14),
        out_specs=tuple(in_vmem(5)),
        compiler_params=params,
        name="backward",
    )(d0, d1, d2, d3, *kept, spec_in, w_in_t, w_out_in)
    return enhanced, grad_first, grad_second, grad_w_in, grad_w_out.T


def exchanged(value, mask):
    pairs = [(source, source ^ mask) for source in range(lax.axis_size("freq"))]
    return lax.ppermute(value, "freq", pairs)


def on_device(features, spectrum, cotangent, w_first, w_second, w_in, w_out):
    frames, bins, channels = features.shape
    block = w_first.shape[1]
    devices = lax.axis_size("freq")
    gathered_bytes = 2 * 2 * devices * frames * bins * channels
    fits = gathered_bytes <= 4 * 2**20
    shaped = (
        block == 2 * bins
        and devices == 2 * block
        and bins <= W_ROWS
        and 2 * block <= LANES
        and LANES < channels
        and 2 * (channels - LANES) == LANES
        and devices % 4 == 0
    )
    plan = whole_rows if fits and shaped else split_rows
    return plan(features, spectrum, cotangent, w_first, w_second, w_in, w_out)


def solution(mesh):
    placed = (
        P("groups", "freq", None),
        P("groups", "freq", None),
        P("groups", "freq", None),
        P("freq", None),
        P("freq", None),
        P(),
        P(),
    )
    return jax.shard_map(
        on_device,
        mesh=mesh,
        in_specs=placed,
        out_specs=(
            P("groups", "freq", None),
            P("freq", "groups"),
            P("freq", "groups"),
            P("groups", None),
            P("groups", None),
        ),
        check_vma=False,
    )
```

```python
import functools
import math

import jax
import jax.numpy as jnp
from jax import lax
from jax.experimental import pallas as pl
from jax.experimental.pallas import tpu as pltpu
from jax.sharding import PartitionSpec as P

gelu_coef = math.sqrt(2.0 / math.pi)


def swapped(value, axis, distance):
    mask = 2**distance
    pairs = [(source, source ^ mask) for source in range(lax.axis_size(axis))]
    return lax.ppermute(value, axis, pairs)


def gelu_pair(pre_act):
    tanh_arg = gelu_coef * (pre_act + 0.044715 * pre_act * pre_act * pre_act)
    tanh_val = jnp.tanh(tanh_arg)
    gelu_out = 0.5 * pre_act * (1.0 + tanh_val)
    gelu_slope = 0.5 * (1.0 + tanh_val) + 0.5 * pre_act * (
        1.0 - tanh_val * tanh_val
    ) * gelu_coef * (1.0 + 3.0 * 0.044715 * pre_act * pre_act)
    return (gelu_out, gelu_slope)


def spread_back(dfirst_two, features):
    frames, own_bins, channels = features.shape
    block = dfirst_two.shape[0]
    quarter = frames // 4
    devices = 2 * block
    send_back = jnp.broadcast_to(dfirst_two[:, None], (block, 2, 2, quarter, channels)).reshape(
        devices, 2 * quarter * channels
    )
    back_rows = lax.all_to_all(send_back, "freq", split_axis=0, concat_axis=0, tiled=True).reshape(
        block, 2, 2, quarter, channels
    )
    by_quarter_x = features.reshape(2, 2, quarter, own_bins, channels)
    return jnp.einsum(
        "hgtbc,pghtc->bp", by_quarter_x, back_rows, preferred_element_type=jnp.float32
    )


def split_rows(features, spectrum, cotangent, w_first, w_second, w_in, w_out):
    frames, own_bins, channels = features.shape
    block = w_first.shape[1]
    quarter = frames // 4
    half_c = channels // 2
    devices = lax.axis_size("freq")
    parity = lax.axis_index("freq") % 2
    lower_side = parity == 0

    def join_halves(mine, theirs, axis):
        return jnp.where(
            lower_side, jnp.concatenate([mine, theirs], axis), jnp.concatenate([theirs, mine], axis)
        )

    got_second = swapped(w_second, "freq", 0)
    full_second = join_halves(w_second, got_second, 0)
    by_quarter = features.reshape(2, 2, quarter, own_bins, channels)
    partials = jnp.einsum(
        "hgtbc,bp->pghtc", by_quarter, w_first, preferred_element_type=jnp.float32
    )
    partials = partials.reshape(devices, 2 * quarter * channels)
    arrived = lax.all_to_all(partials, "freq", split_axis=0, concat_axis=0, tiled=True)
    first_two = arrived.reshape(block, 2, 2, quarter, channels).sum(axis=1).astype(jnp.bfloat16)
    spectral = jnp.einsum(
        "ahtc,aq->htqc", first_two, full_second, preferred_element_type=jnp.float32
    ).astype(jnp.bfloat16)
    flat_rows = spectral.reshape(-1, channels)
    pre_act = jnp.dot(flat_rows, w_in, preferred_element_type=jnp.float32)
    gelu_out, gelu_slope = gelu_pair(pre_act)
    hidden = gelu_out.astype(jnp.bfloat16)
    spectral_mask = (
        flat_rows.astype(jnp.float32) + jnp.dot(hidden, w_out, preferred_element_type=jnp.float32)
    ).astype(jnp.bfloat16)
    spectral_mask = spectral_mask.reshape(2, quarter, block, channels)
    send_mask = lax.dynamic_slice_in_dim(spectral_mask, (1 - parity) * own_bins, own_bins, 2)
    keep_mask = lax.dynamic_slice_in_dim(spectral_mask, parity * own_bins, own_bins, 2)
    got_mask = swapped(send_mask, "freq", 0)
    full_mask = jnp.where(
        lower_side, jnp.stack([keep_mask, got_mask], 1), jnp.stack([got_mask, keep_mask], 1)
    )
    mask_f = full_mask.reshape(frames, own_bins, channels).astype(jnp.float32)
    spec_f = spectrum.astype(jnp.float32)
    mask_re, mask_im = (mask_f[..., :half_c], mask_f[..., half_c:])
    spec_re, spec_im = (spec_f[..., :half_c], spec_f[..., half_c:])
    enhanced = jnp.concatenate(
        [spec_re * mask_re - spec_im * mask_im, spec_re * mask_im + spec_im * mask_re], -1
    ).astype(jnp.bfloat16)
    loss_scale = jnp.float32(1.0) / jnp.sqrt(jnp.float32(frames * devices * own_bins))
    grad_f = cotangent.astype(jnp.float32) * loss_scale
    grad_re, grad_im = (grad_f[..., :half_c], grad_f[..., half_c:])
    dmask = jnp.concatenate(
        [grad_re * spec_re + grad_im * spec_im, grad_im * spec_re - grad_re * spec_im], -1
    ).astype(jnp.bfloat16)
    dmask = dmask.reshape(2, 2, quarter, own_bins, channels)
    send_dmask = lax.dynamic_index_in_dim(dmask, 1 - parity, 1, keepdims=False)
    keep_dmask = lax.dynamic_index_in_dim(dmask, parity, 1, keepdims=False)
    got_dmask = swapped(send_dmask, "freq", 0)
    dmask_rows = join_halves(keep_dmask, got_dmask, 2).reshape(-1, channels)
    dact = jnp.dot(dmask_rows, w_out.T, preferred_element_type=jnp.float32)
    dpre = (dact * gelu_slope).astype(jnp.bfloat16)
    part_out = jnp.dot(hidden.T, dmask_rows, preferred_element_type=jnp.float32)
    part_in = jnp.dot(flat_rows.T, dpre, preferred_element_type=jnp.float32)
    grad_w_in, grad_w_out = lax.psum((part_in, part_out), "freq")
    dspectral = (
        dmask_rows.astype(jnp.float32) + jnp.dot(dpre, w_in.T, preferred_element_type=jnp.float32)
    ).astype(jnp.bfloat16)
    dspectral = dspectral.reshape(2, quarter, block, channels)
    dfirst_two = jnp.einsum(
        "htqc,aq->ahtc", dspectral, full_second, preferred_element_type=jnp.float32
    ).astype(jnp.bfloat16)
    second_part = jnp.einsum(
        "ahtc,htqc->aq", first_two, dspectral, preferred_element_type=jnp.float32
    )
    second_part = second_part.reshape(2, own_bins, block)
    got_part = swapped(
        lax.dynamic_index_in_dim(second_part, 1 - parity, 0, keepdims=False), "freq", 0
    )
    grad_second = lax.dynamic_index_in_dim(second_part, parity, 0, keepdims=False) + got_part
    grad_first = spread_back(dfirst_two, features)
    return (enhanced, grad_first, grad_second, grad_w_in, grad_w_out)


f32, bf16 = jnp.float32, jnp.bfloat16
NN = (((1,), (0,)), ((), ()))
NT = (((1,), (1,)), ((), ()))
TN = (((0,), (0,)), ((), ()))
LANES = 128
W_ROWS = 16


def mul(a, b, dims=NN):
    return lax.dot_general(a, b, dims, preferred_element_type=f32)


def mul_f32(a, b):
    return lax.dot_general(a, b, NN, precision=lax.Precision.HIGHEST, preferred_element_type=f32)


def iota(shape, dim):
    return lax.broadcasted_iota(jnp.int32, shape, dim)


def onehot(cond):
    return cond.astype(f32).astype(bf16)


def gelu_and_slope(v):
    square = v * v
    tanh_val = jnp.tanh(v * (gelu_coef + (gelu_coef * 0.044715) * square))
    half = 0.5 + 0.5 * tanh_val
    out = v * half
    slope = half + out * (1.0 - half) * (
        2.0 * gelu_coef + (6.0 * gelu_coef * 0.044715) * square
    )
    return out, slope


class Rows:
    def __init__(self, own, bins, rows):
        self.own, self.bins, self.per_block = own, bins, 2 * own
        self.half = rows // (2 * self.per_block)
        me = lax.axis_index("freq")
        self.chip, self.side = me >> 1, (me & 1) * bins

    def local(self, r):
        return r // self.per_block

    def block(self, r):
        k = self.local(r)
        return ((k & (self.half - 1)) << 1) | (k // self.half)

    def place(self, r):
        return ((r // self.own) & 1) * self.bins + (r & (self.bins - 1))

    def frame(self, r):
        return (r // self.bins) & (self.own // self.bins - 1)


def pack_rows(rows):
    half = rows.shape[0] // 2
    low, high = rows[:half], rows[half:]
    rest = jnp.concatenate([low[:, LANES:], high[:, LANES:]], 1)
    return low[:, :LANES], high[:, :LANES], rest


def unpacked(low, high, rest):
    split = rest.shape[1] // 2
    return (
        jnp.concatenate([low, rest[:, :split]], 1),
        jnp.concatenate([high, rest[:, split:]], 1),
    )


def cut(value):
    return value[:, :LANES], value[:, LANES : 2 * LANES], value[:, 2 * LANES :]


def received_from(devices):
    column = [*range(devices - 4, 0, -4)]
    near, far = [*column, 0, 2], [j ^ 2 for j in column]
    return [near, [j ^ 1 for j in near], far, [j ^ 1 for j in far]]


def piece(refs, per_device, devices, j, start, size):
    held = received_from(devices)
    n = next(n for n, part in enumerate(held) if j in part)
    at = held[n].index(j) * per_device + start
    return refs[n][at : at + size, :]


def halves_of(devices):
    return [[j for j in range(devices) if j & 2 == bit] for bit in (0, 2)]


def tiles_of(refs, per_device, devices, own, order):
    return [
        jnp.concatenate([piece(refs, per_device, devices, j, t * own, own) for j in order], 0)
        for t in range(3)
    ]


def pack_kernel(
    x_hbm, s_hbm, c_hbm, w1_hbm, w2_hbm, w_in_hbm, w_out_hbm,
    out_ref, s_ref, w_in_ref, w_out_ref,
    x_ref, c_ref, w1_ref, w2_ref, sems, *, scale,
):
    copies = [
        pltpu.make_async_copy(src, dst, sems.at[n])
        for n, (src, dst) in enumerate(
            [
                (x_hbm, x_ref),
                (w1_hbm, w1_ref),
                (w2_hbm, w2_ref),
                (s_hbm, s_ref),
                (c_hbm, c_ref),
                (w_in_hbm, w_in_ref),
                (w_out_hbm, w_out_ref),
            ]
        )
    ]
    for copy in copies:
        copy.start()
    for copy in copies[:3]:
        copy.wait()
    frames, bins, channels = x_ref.shape
    rows = frames * bins
    half = rows // 2
    half_c = channels // 2
    block = w1_ref.shape[1]

    for t, part in enumerate(pack_rows(x_ref[...].astype(f32).reshape(rows, channels))):
        out_ref[t * half : (t + 1) * half, :] = part.astype(bf16)
    weights = jnp.concatenate([w1_ref[...].astype(f32), w2_ref[...].astype(f32)], 1)
    weights = jnp.concatenate([weights, jnp.zeros((bins, LANES - 2 * block), f32)], 1)
    weights = jnp.concatenate([weights, jnp.zeros((W_ROWS - bins, LANES), f32)], 0)
    start = 3 * half + W_ROWS
    out_ref[3 * half : start, :] = weights.astype(bf16)

    for copy in copies[3:5]:
        copy.wait()
    spec = s_ref[...].astype(f32).reshape(rows, channels)
    grad = c_ref[...].astype(f32).reshape(rows, channels) * scale
    spec_re, spec_im = spec[:, :half_c], spec[:, half_c:]
    grad_re, grad_im = grad[:, :half_c], grad[:, half_c:]
    dmask = jnp.concatenate(
        [grad_re * spec_re + grad_im * spec_im, grad_im * spec_re - grad_re * spec_im], 1
    )
    for t, part in enumerate(pack_rows(dmask)):
        out_ref[start + t * half : start + (t + 1) * half, :] = part.astype(bf16)
    for copy in copies[5:]:
        copy.wait()


def prepare_kernel(
    own_ref, w_in_ref, x_ref, d_ref, w_in_t_ref, valid_ref, pick1_ref, spread1_ref, keep1_ref,
    pick2_ref, spread2_ref, keep2_ref, chosen_ref, *, bins,
):
    w_in_t_ref[...] = w_in_ref[...].T
    x_ref[...] = own_ref[: x_ref.shape[0], :]
    d_ref[...] = own_ref[x_ref.shape[0] :, :]
    own, rows = chosen_ref.shape
    block = 2 * bins
    at = Rows(own, bins, rows)

    def w_place(r):
        return ((r // W_ROWS) & 1) * bins + (r & (W_ROWS - 1))

    def w_block(r):
        return r // (2 * W_ROWS)

    r, w = iota(valid_ref.shape, 0), iota(valid_ref.shape, 1)
    valid_ref[...] = onehot(((w & (W_ROWS - 1)) < bins) & (w_block(w) == at.local(r)))

    r, lane = iota(pick1_ref.shape, 0), iota(pick1_ref.shape, 1)
    pick1_ref[...] = onehot(lane == at.place(r))
    pick2_ref[...] = onehot(lane == block + (at.place(r) ^ at.side))

    w, r = iota(spread1_ref.shape, 0), iota(spread1_ref.shape, 1)
    spread1_ref[...] = onehot((w_place(w) == at.place(r)) & (w_block(w) == at.local(r)))
    w, r = iota(spread2_ref.shape, 0), iota(spread2_ref.shape, 1)
    spread2_ref[...] = onehot(w_place(w) == (at.block(r) ^ at.chip ^ at.side))

    row, col = iota(keep1_ref.shape, 0), iota(keep1_ref.shape, 1)
    keep1_ref[...] = onehot(at.frame(row) == at.frame(col))
    row, col = iota(keep2_ref.shape, 0), iota(keep2_ref.shape, 1)
    keep2_ref[...] = onehot(
        (at.frame(row) == at.frame(col)) & (at.place(col) == (at.block(row) ^ at.chip))
    )

    row, col = iota(chosen_ref.shape, 0), iota(chosen_ref.shape, 1)
    chosen_ref[...] = onehot(
        (at.block(col) == ((at.side + (row & (bins - 1))) ^ at.chip))
        & (at.place(col) == at.chip)
        & (at.frame(row) == at.frame(col))
    )


def mixing(refs, devices, own, order, selections, keep2):
    valid_ref, pick1_ref, spread1_ref, keep1_ref, pick2_ref, spread2_ref = selections
    per_x = 3 * own + W_ROWS
    factors = jnp.concatenate(
        [piece(refs, per_x, devices, j, 3 * own, W_ROWS) for j in order], 0
    )
    tiles = tiles_of(refs, per_x, devices, own, order)
    picked = [
        mul(pick[...], factors, NT).astype(bf16) * valid_ref[...] for pick in (pick1_ref, pick2_ref)
    ]
    mix1 = mul(picked[0], spread1_ref[...]).astype(bf16) * keep1_ref[...]
    mix2 = mul(picked[1], spread2_ref[...]).astype(bf16) * keep2
    return tiles, mul(mix1, jnp.concatenate(tiles, 1)).astype(bf16), mix2


def near_kernel(
    x0, x1, valid_ref, pick1_ref, spread1_ref, keep1_ref, pick2_ref, spread2_ref, keep2_ref,
    first_ref, mix2_ref, part_ref, own_ref, mark_ref,
):
    own = own_ref.shape[0] // 2
    half, rows = mix2_ref.shape
    devices = rows // own
    selections = (valid_ref, pick1_ref, spread1_ref, keep1_ref, pick2_ref, spread2_ref)
    tiles, first, mix2 = mixing(
        (x0, x1), devices, own, halves_of(devices)[0], selections, keep2_ref[:half, :]
    )
    first_ref[...] = first
    mix2_ref[...] = mix2
    part_ref[...] = mul(mix2[:, :half], first)
    own_ref[:own, :], own_ref[own:, :] = unpacked(*[tile[:own] for tile in tiles])
    mark_ref[...] = jnp.zeros_like(mark_ref)


def mix_kernel(
    x2, x3, x0, x1, first_near_ref, mix2_near_ref, part_ref,
    valid_ref, pick1_ref, spread1_ref, keep1_ref,
    pick2_ref, spread2_ref, keep2_ref, chosen_ref,
    sp_ref, back_ref, first_ref, sp_own_ref, mark_ref,
):
    own = sp_own_ref.shape[0] // 2
    half, rows = mix2_near_ref.shape
    devices = rows // own
    selections = (valid_ref, pick1_ref, spread1_ref, keep1_ref, pick2_ref, spread2_ref)
    _, first_far, mix2_far = mixing(
        (x0, x1, x2, x3), devices, own, halves_of(devices)[1], selections, keep2_ref[half:, :]
    )
    first = jnp.concatenate([first_near_ref[...], first_far], 0)
    spectral = jnp.concatenate(
        [
            (part_ref[...] + mul(mix2_near_ref[:, half:], first_far)).astype(bf16),
            mul(mix2_far, first).astype(bf16),
        ],
        0,
    )
    back_ref[:half, :] = mix2_near_ref[:, : 2 * own]
    back_ref[half:, :] = mix2_far[:, : 2 * own]
    sp_low, sp_high = unpacked(*cut(spectral))
    sp_own_ref[:own, :], sp_own_ref[own:, :] = sp_low[:own], sp_high[:own]
    first_ref[:own, :], first_ref[own:, :] = unpacked(
        *cut(mul(chosen_ref[...], first).astype(bf16))
    )

    sp_ref[:rows, :] = sp_low
    sp_ref[rows:, :] = sp_high
    mark_ref[...] = jnp.zeros_like(mark_ref)


def hidden_kernel(sp_ref, w_in_ref, hid_ref, slope_ref, spt_ref):
    sp = sp_ref[...]
    gelu_out, slope = gelu_and_slope(mul(sp, w_in_ref[...]))
    hid_ref[...] = gelu_out.astype(bf16)
    slope_ref[...] = slope
    spt_ref[...] = sp.T


def backward_kernel(
    hid_ref, slope_ref, spt_ref, back_ref, first_ref, sp_own_ref, own_ref, d2, d0, d1, d3,
    s_ref, w_in_t_ref, w_out_ref,
    enh_ref, g1_ref, g2_ref, gwi_ref, gwo_ref,
):
    bins, block = g1_ref.shape
    frames, _, channels = s_ref.shape
    half_c = channels // 2
    own = own_ref.shape[0] // 2
    refs = (d0, d1, d2, d3)
    rows = hid_ref.shape[0] // 2
    devices = rows // own
    at = Rows(own, bins, rows)
    order = sum(halves_of(devices), [])
    dm_low, dm_high = unpacked(*tiles_of(refs, 3 * own, devices, own, order))
    dpre, dsp = [], []
    for n, part in enumerate((dm_low, dm_high)):
        to = slice(n * rows, (n + 1) * rows)
        dpre.append((mul(part, w_out_ref[...]) * slope_ref[to, :]).astype(bf16))
    for n, part in enumerate((dm_low, dm_high)):
        dsp.append((part.astype(f32) + mul(dpre[n], w_in_t_ref[...])).astype(bf16))
    gwi_ref[...] = mul(spt_ref[:, :rows], dpre[0]) + mul(spt_ref[:, rows:], dpre[1])
    gwo_ref[...] = mul(dm_low, hid_ref[:rows, :], TN) + mul(dm_high, hid_ref[rows:, :], TN)

    sp_own = sp_own_ref[...]
    hidden = jnp.concatenate([hid_ref[:own, :], hid_ref[rows : rows + own, :]], 0)
    mask = (sp_own.astype(f32) + mul(hidden, w_out_ref[...], NT)).astype(bf16).astype(f32)
    spec = s_ref[...].astype(f32).reshape(2 * own, channels)
    spec_re, spec_im = spec[:, :half_c], spec[:, half_c:]
    mask_re, mask_im = mask[:, :half_c], mask[:, half_c:]
    enhanced = jnp.concatenate(
        [spec_re * mask_re - spec_im * mask_im, spec_re * mask_im + spec_im * mask_re], 1
    )
    enh_ref[...] = enhanced.reshape(frames, bins, channels).astype(bf16)

    dsp_low, dsp_high = dsp
    dfirst_low = mul(back_ref[...], dsp_low, TN).astype(bf16)
    dfirst_high = mul(back_ref[...], dsp_high, TN).astype(bf16)

    per_block = at.per_block
    frames_meet = at.frame(iota((own, per_block), 0)) == at.frame(iota((own, per_block), 1))

    def bin_sums(gram):
        parts = jnp.where(frames_meet, gram, 0.0)
        total = sum(parts[n : n + 2 * bins] for n in range(0, own, 2 * bins))
        return total[:bins] + total[bins:]

    gram = mul(own_ref[:own, :], dfirst_low, NT) + mul(own_ref[own:, :], dfirst_high, NT)
    sums = [bin_sums(gram)]
    gram = mul(first_ref[:own, :], dsp_low[:per_block], NT)
    gram += mul(first_ref[own:, :], dsp_high[:per_block], NT)
    sums.append(bin_sums(gram))
    row, col = iota((2 * per_block, 2 * block), 0), iota((2 * per_block, 2 * block), 1)
    place = at.place(row & (per_block - 1))
    take = ((row < per_block) & (place == col)) | (
        (row >= per_block) & (block + (place ^ at.side) == col)
    )
    both = mul_f32(jnp.concatenate(sums, 1), take.astype(f32))
    g1_ref[...] = both[:, :block]
    g2_ref[...] = both[:, block:]


def whole_rows(features, spectrum, cotangent, w_first, w_second, w_in, w_out):
    frames, bins, channels = features.shape
    block = w_first.shape[1]
    hid = w_in.shape[1]
    devices = lax.axis_size("freq")
    own = frames // 2 * bins
    rows = devices * own
    in_vmem = lambda n: [pl.BlockSpec(memory_space=pltpu.VMEM)] * n
    in_hbm = lambda n: [pl.BlockSpec(memory_space=pltpu.HBM)] * n
    shaped = jax.ShapeDtypeStruct
    params = pltpu.CompilerParams(vmem_limit_bytes=40 * 2**20)
    scale = 1.0 / math.sqrt(frames * devices * bins)
    own_rows, spec_in, w_in_in, w_out_in = pl.pallas_call(
        functools.partial(pack_kernel, scale=scale),
        out_shape=(
            pltpu.VMEM((6 * own + W_ROWS, LANES), bf16),
            pltpu.VMEM((frames, bins, channels), bf16),
            pltpu.VMEM((channels, hid), bf16),
            pltpu.VMEM((channels, hid), bf16),
        ),
        in_specs=in_hbm(7),
        out_specs=tuple(in_vmem(4)),
        scratch_shapes=[
            pltpu.VMEM((frames, bins, channels), bf16),
            pltpu.VMEM((frames, bins, channels), bf16),
            pltpu.VMEM((bins, block), bf16),
            pltpu.VMEM((bins, block), bf16),
            pltpu.SemaphoreType.DMA((7,)),
        ],
        name="pack",
    )(features, spectrum, cotangent, w_first, w_second, w_in, w_out.T)
    w_rows = devices * W_ROWS
    x_own, d_own, w_in_t, *selections = pl.pallas_call(
        functools.partial(prepare_kernel, bins=bins),
        out_shape=tuple(
            pltpu.VMEM(shape, bf16)
            for shape in [
                (3 * own + W_ROWS, LANES),
                (3 * own, LANES),
                (hid, channels),
                (rows // 2, w_rows // 2),
                (rows // 2, LANES),
                (w_rows // 2, rows // 2),
                (rows // 2, rows // 2),
                (rows // 2, LANES),
                (w_rows // 2, rows),
                (rows, rows),
                (own, rows),
            ]
        ),
        in_specs=in_vmem(2),
        out_specs=tuple(in_vmem(11)),
        compiler_params=params,
        cost_estimate=pl.CostEstimate(flops=0, bytes_accessed=2**21, transcendentals=0),
        name="prepare",
    )(own_rows, w_in_in)

    column = [exchanged(own_rows, j) for j in range(devices - 4, 0, -4)]
    x_rows = 3 * own + W_ROWS
    across = exchanged(own_rows, 2)
    x_column = jnp.concatenate([got[:x_rows] for got in column], 0)
    d_column = jnp.concatenate([got[x_rows:] for got in column], 0)
    x2, d2 = exchanged(x_column, 2), exchanged(d_column, 2)
    x0 = jnp.concatenate([x_column, x_own, across[:x_rows]], 0)
    d0 = jnp.concatenate([d_column, d_own, across[x_rows:]], 0)
    x1, d1 = exchanged(x0, 1), exchanged(d0, 1)
    first_near, mix2_near, part, x_rows_own, mark = pl.pallas_call(
        near_kernel,
        out_shape=(
            pltpu.VMEM((rows // 2, 2 * channels), bf16),
            pltpu.VMEM((rows // 2, rows), bf16),
            pltpu.VMEM((rows // 2, 2 * channels), f32),
            pltpu.VMEM((2 * own, channels), bf16),
            pltpu.VMEM((W_ROWS, LANES), bf16),
        ),
        in_specs=in_vmem(9),
        out_specs=tuple(in_vmem(5)),
        compiler_params=params,
        name="near",
    )(x0, x1, *selections[:-1])
    x3 = exchanged(jnp.concatenate([x2, mark], 0), 1)
    spectral, *kept, mark = pl.pallas_call(
        mix_kernel,
        out_shape=tuple(
            pltpu.VMEM(shape, bf16)
            for shape in [
                (2 * rows, channels),
                (rows, 2 * own),
                (2 * own, channels),
                (2 * own, channels),
                (W_ROWS, LANES),
            ]
        ),
        in_specs=in_vmem(15),
        out_specs=tuple(in_vmem(5)),
        compiler_params=params,
        name="mix",
    )(x2, x3, x0, x1, first_near, mix2_near, part, *selections)
    d3 = exchanged(jnp.concatenate([d2, mark], 0), 1)
    hidden = pl.pallas_call(
        hidden_kernel,
        out_shape=(
            pltpu.VMEM((2 * rows, hid), bf16),
            pltpu.VMEM((2 * rows, hid), f32),
            pltpu.VMEM((channels, 2 * rows), bf16),
        ),
        in_specs=in_vmem(2),
        out_specs=tuple(in_vmem(3)),
        compiler_params=params,
        name="hidden",
    )(spectral, w_in_in)

    enhanced, grad_first, grad_second, grad_w_in, grad_w_out = pl.pallas_call(
        backward_kernel,
        out_shape=(
            shaped((frames, bins, channels), bf16),
            shaped((bins, block), f32),
            shaped((bins, block), f32),
            shaped((channels, hid), f32),
            shaped((channels, hid), f32),
        ),
        in_specs=in_vmem(14),
        out_specs=tuple(in_vmem(5)),
        compiler_params=params,
        name="backward",
    )(*hidden, *kept, x_rows_own, d2, d0, d1, d3, spec_in, w_in_t, w_out_in)
    return enhanced, grad_first, grad_second, grad_w_in, grad_w_out.T


def exchanged(value, mask):
    pairs = [(source, source ^ mask) for source in range(lax.axis_size("freq"))]
    return lax.ppermute(value, "freq", pairs)


def on_device(features, spectrum, cotangent, w_first, w_second, w_in, w_out):
    frames, bins, channels = features.shape
    block = w_first.shape[1]
    devices = lax.axis_size("freq")
    gathered_bytes = 2 * 2 * devices * frames * bins * channels
    fits = gathered_bytes <= 4 * 2**20
    shaped = (
        block == 2 * bins
        and devices == 2 * block
        and bins <= W_ROWS
        and 2 * block <= LANES
        and LANES < channels
        and 2 * (channels - LANES) == LANES
        and devices % 4 == 0
    )
    plan = whole_rows if fits and shaped else split_rows
    return plan(features, spectrum, cotangent, w_first, w_second, w_in, w_out)


def solution(mesh):
    placed = (
        P("groups", "freq", None),
        P("groups", "freq", None),
        P("groups", "freq", None),
        P("freq", None),
        P("freq", None),
        P(),
        P(),
    )
    return jax.shard_map(
        on_device,
        mesh=mesh,
        in_specs=placed,
        out_specs=(
            P("groups", "freq", None),
            P("freq", "groups"),
            P("freq", "groups"),
            P("groups", None),
            P("groups", None),
        ),
        check_vma=False,
    )
```

```python
import functools
import math

import jax
import jax.numpy as jnp
from jax import lax
from jax.experimental import pallas as pl
from jax.experimental.pallas import tpu as pltpu
from jax.sharding import PartitionSpec as P

gelu_coef = math.sqrt(2.0 / math.pi)


def swapped(value, axis, distance):
    mask = 2**distance
    pairs = [(source, source ^ mask) for source in range(lax.axis_size(axis))]
    return lax.ppermute(value, axis, pairs)


def gelu_pair(pre_act):
    tanh_arg = gelu_coef * (pre_act + 0.044715 * pre_act * pre_act * pre_act)
    tanh_val = jnp.tanh(tanh_arg)
    gelu_out = 0.5 * pre_act * (1.0 + tanh_val)
    gelu_slope = 0.5 * (1.0 + tanh_val) + 0.5 * pre_act * (
        1.0 - tanh_val * tanh_val
    ) * gelu_coef * (1.0 + 3.0 * 0.044715 * pre_act * pre_act)
    return (gelu_out, gelu_slope)


def spread_back(dfirst_two, features):
    frames, own_bins, channels = features.shape
    block = dfirst_two.shape[0]
    quarter = frames // 4
    devices = 2 * block
    send_back = jnp.broadcast_to(dfirst_two[:, None], (block, 2, 2, quarter, channels)).reshape(
        devices, 2 * quarter * channels
    )
    back_rows = lax.all_to_all(send_back, "freq", split_axis=0, concat_axis=0, tiled=True).reshape(
        block, 2, 2, quarter, channels
    )
    by_quarter_x = features.reshape(2, 2, quarter, own_bins, channels)
    return jnp.einsum(
        "hgtbc,pghtc->bp", by_quarter_x, back_rows, preferred_element_type=jnp.float32
    )


def split_rows(features, spectrum, cotangent, w_first, w_second, w_in, w_out):
    frames, own_bins, channels = features.shape
    block = w_first.shape[1]
    quarter = frames // 4
    half_c = channels // 2
    devices = lax.axis_size("freq")
    parity = lax.axis_index("freq") % 2
    lower_side = parity == 0

    def join_halves(mine, theirs, axis):
        return jnp.where(
            lower_side, jnp.concatenate([mine, theirs], axis), jnp.concatenate([theirs, mine], axis)
        )

    got_second = swapped(w_second, "freq", 0)
    full_second = join_halves(w_second, got_second, 0)
    by_quarter = features.reshape(2, 2, quarter, own_bins, channels)
    partials = jnp.einsum(
        "hgtbc,bp->pghtc", by_quarter, w_first, preferred_element_type=jnp.float32
    )
    partials = partials.reshape(devices, 2 * quarter * channels)
    arrived = lax.all_to_all(partials, "freq", split_axis=0, concat_axis=0, tiled=True)
    first_two = arrived.reshape(block, 2, 2, quarter, channels).sum(axis=1).astype(jnp.bfloat16)
    spectral = jnp.einsum(
        "ahtc,aq->htqc", first_two, full_second, preferred_element_type=jnp.float32
    ).astype(jnp.bfloat16)
    flat_rows = spectral.reshape(-1, channels)
    pre_act = jnp.dot(flat_rows, w_in, preferred_element_type=jnp.float32)
    gelu_out, gelu_slope = gelu_pair(pre_act)
    hidden = gelu_out.astype(jnp.bfloat16)
    spectral_mask = (
        flat_rows.astype(jnp.float32) + jnp.dot(hidden, w_out, preferred_element_type=jnp.float32)
    ).astype(jnp.bfloat16)
    spectral_mask = spectral_mask.reshape(2, quarter, block, channels)
    send_mask = lax.dynamic_slice_in_dim(spectral_mask, (1 - parity) * own_bins, own_bins, 2)
    keep_mask = lax.dynamic_slice_in_dim(spectral_mask, parity * own_bins, own_bins, 2)
    got_mask = swapped(send_mask, "freq", 0)
    full_mask = jnp.where(
        lower_side, jnp.stack([keep_mask, got_mask], 1), jnp.stack([got_mask, keep_mask], 1)
    )
    mask_f = full_mask.reshape(frames, own_bins, channels).astype(jnp.float32)
    spec_f = spectrum.astype(jnp.float32)
    mask_re, mask_im = (mask_f[..., :half_c], mask_f[..., half_c:])
    spec_re, spec_im = (spec_f[..., :half_c], spec_f[..., half_c:])
    enhanced = jnp.concatenate(
        [spec_re * mask_re - spec_im * mask_im, spec_re * mask_im + spec_im * mask_re], -1
    ).astype(jnp.bfloat16)
    loss_scale = jnp.float32(1.0) / jnp.sqrt(jnp.float32(frames * devices * own_bins))
    grad_f = cotangent.astype(jnp.float32) * loss_scale
    grad_re, grad_im = (grad_f[..., :half_c], grad_f[..., half_c:])
    dmask = jnp.concatenate(
        [grad_re * spec_re + grad_im * spec_im, grad_im * spec_re - grad_re * spec_im], -1
    ).astype(jnp.bfloat16)
    dmask = dmask.reshape(2, 2, quarter, own_bins, channels)
    send_dmask = lax.dynamic_index_in_dim(dmask, 1 - parity, 1, keepdims=False)
    keep_dmask = lax.dynamic_index_in_dim(dmask, parity, 1, keepdims=False)
    got_dmask = swapped(send_dmask, "freq", 0)
    dmask_rows = join_halves(keep_dmask, got_dmask, 2).reshape(-1, channels)
    dact = jnp.dot(dmask_rows, w_out.T, preferred_element_type=jnp.float32)
    dpre = (dact * gelu_slope).astype(jnp.bfloat16)
    part_out = jnp.dot(hidden.T, dmask_rows, preferred_element_type=jnp.float32)
    part_in = jnp.dot(flat_rows.T, dpre, preferred_element_type=jnp.float32)
    grad_w_in, grad_w_out = lax.psum((part_in, part_out), "freq")
    dspectral = (
        dmask_rows.astype(jnp.float32) + jnp.dot(dpre, w_in.T, preferred_element_type=jnp.float32)
    ).astype(jnp.bfloat16)
    dspectral = dspectral.reshape(2, quarter, block, channels)
    dfirst_two = jnp.einsum(
        "htqc,aq->ahtc", dspectral, full_second, preferred_element_type=jnp.float32
    ).astype(jnp.bfloat16)
    second_part = jnp.einsum(
        "ahtc,htqc->aq", first_two, dspectral, preferred_element_type=jnp.float32
    )
    second_part = second_part.reshape(2, own_bins, block)
    got_part = swapped(
        lax.dynamic_index_in_dim(second_part, 1 - parity, 0, keepdims=False), "freq", 0
    )
    grad_second = lax.dynamic_index_in_dim(second_part, parity, 0, keepdims=False) + got_part
    grad_first = spread_back(dfirst_two, features)
    return (enhanced, grad_first, grad_second, grad_w_in, grad_w_out)


f32, bf16 = jnp.float32, jnp.bfloat16
NN = (((1,), (0,)), ((), ()))
NT = (((1,), (1,)), ((), ()))
TN = (((0,), (0,)), ((), ()))
LANES = 128
W_ROWS = 16


def mul(a, b, dims=NN):
    return lax.dot_general(a, b, dims, preferred_element_type=f32)


def mul_f32(a, b):
    return lax.dot_general(a, b, NN, precision=lax.Precision.HIGHEST, preferred_element_type=f32)


def iota(shape, dim):
    return lax.broadcasted_iota(jnp.int32, shape, dim)


def onehot(cond):
    return cond.astype(f32).astype(bf16)


def gelu_and_slope(v):
    square = v * v
    tanh_val = jnp.tanh(v * (gelu_coef + (gelu_coef * 0.044715) * square))
    half = 0.5 + 0.5 * tanh_val
    out = v * half
    slope = half + out * (1.0 - half) * (
        2.0 * gelu_coef + (6.0 * gelu_coef * 0.044715) * square
    )
    return out, slope


class Rows:
    def __init__(self, own, bins, rows):
        self.own, self.bins, self.per_block = own, bins, 2 * own
        self.half = rows // (2 * self.per_block)
        me = lax.axis_index("freq")
        self.chip, self.side = me >> 1, (me & 1) * bins

    def local(self, r):
        return r // self.per_block

    def block(self, r):
        k = self.local(r)
        return ((k & (self.half - 1)) << 1) | (k // self.half)

    def place(self, r):
        return ((r // self.own) & 1) * self.bins + (r & (self.bins - 1))

    def frame(self, r):
        return (r // self.bins) & (self.own // self.bins - 1)


def pack_rows(rows):
    half = rows.shape[0] // 2
    low, high = rows[:half], rows[half:]
    rest = jnp.concatenate([low[:, LANES:], high[:, LANES:]], 1)
    return low[:, :LANES], high[:, :LANES], rest


def unpacked(low, high, rest):
    split = rest.shape[1] // 2
    return (
        jnp.concatenate([low, rest[:, :split]], 1),
        jnp.concatenate([high, rest[:, split:]], 1),
    )


def cut(value):
    return value[:, :LANES], value[:, LANES : 2 * LANES], value[:, 2 * LANES :]


def received_from(devices):
    column = [*range(devices - 4, 0, -4)]
    near, far = [*column, 0, 2], [j ^ 2 for j in column]
    return [near, [j ^ 1 for j in near], far, [j ^ 1 for j in far]]


def piece(refs, per_device, devices, j, start, size):
    held = received_from(devices)
    n = next(n for n, part in enumerate(held) if j in part)
    at = held[n].index(j) * per_device + start
    return refs[n][at : at + size, :]


def halves_of(devices):
    return [[j for j in range(devices) if j & 2 == bit] for bit in (0, 2)]


def tiles_of(refs, per_device, devices, own, order):
    return [
        jnp.concatenate([piece(refs, per_device, devices, j, t * own, own) for j in order], 0)
        for t in range(3)
    ]


def pack_kernel(
    x_hbm, s_hbm, c_hbm, w1_hbm, w2_hbm, w_in_hbm, w_out_hbm,
    out_ref, s_ref, w_in_ref, w_out_ref,
    x_ref, c_ref, w1_ref, w2_ref, sems, *, scale,
):
    copies = [
        pltpu.make_async_copy(src, dst, sems.at[n])
        for n, (src, dst) in enumerate(
            [
                (x_hbm, x_ref),
                (w1_hbm, w1_ref),
                (w2_hbm, w2_ref),
                (s_hbm, s_ref),
                (c_hbm, c_ref),
                (w_in_hbm, w_in_ref),
                (w_out_hbm, w_out_ref),
            ]
        )
    ]
    for copy in copies:
        copy.start()
    for copy in copies[:3]:
        copy.wait()
    frames, bins, channels = x_ref.shape
    rows = frames * bins
    half = rows // 2
    half_c = channels // 2
    block = w1_ref.shape[1]

    for t, part in enumerate(pack_rows(x_ref[...].astype(f32).reshape(rows, channels))):
        out_ref[t * half : (t + 1) * half, :] = part.astype(bf16)
    weights = jnp.concatenate([w1_ref[...].astype(f32), w2_ref[...].astype(f32)], 1)
    weights = jnp.concatenate([weights, jnp.zeros((bins, LANES - 2 * block), f32)], 1)
    weights = jnp.concatenate([weights, jnp.zeros((W_ROWS - bins, LANES), f32)], 0)
    start = 3 * half + W_ROWS
    out_ref[3 * half : start, :] = weights.astype(bf16)

    for copy in copies[3:5]:
        copy.wait()
    spec = s_ref[...].astype(f32).reshape(rows, channels)
    grad = c_ref[...].astype(f32).reshape(rows, channels) * scale
    spec_re, spec_im = spec[:, :half_c], spec[:, half_c:]
    grad_re, grad_im = grad[:, :half_c], grad[:, half_c:]
    dmask = jnp.concatenate(
        [grad_re * spec_re + grad_im * spec_im, grad_im * spec_re - grad_re * spec_im], 1
    )
    for t, part in enumerate(pack_rows(dmask)):
        out_ref[start + t * half : start + (t + 1) * half, :] = part.astype(bf16)
    for copy in copies[5:]:
        copy.wait()


def prepare_kernel(
    own_ref, w_in_ref, x_ref, d_ref, w_in_t_ref, valid_ref, pick1_ref, spread1_ref, keep1_ref,
    pick2_ref, spread2_ref, keep2_ref, chosen_ref, *, bins,
):
    w_in_t_ref[...] = w_in_ref[...].T
    x_ref[...] = own_ref[: x_ref.shape[0], :]
    d_ref[...] = own_ref[x_ref.shape[0] :, :]
    own, rows = chosen_ref.shape
    block = 2 * bins
    at = Rows(own, bins, rows)

    def w_place(r):
        return ((r // W_ROWS) & 1) * bins + (r & (W_ROWS - 1))

    def w_block(r):
        return r // (2 * W_ROWS)

    r, w = iota(valid_ref.shape, 0), iota(valid_ref.shape, 1)
    valid_ref[...] = onehot(((w & (W_ROWS - 1)) < bins) & (w_block(w) == at.local(r)))

    r, lane = iota(pick1_ref.shape, 0), iota(pick1_ref.shape, 1)
    pick1_ref[...] = onehot(lane == at.place(r))
    pick2_ref[...] = onehot(lane == block + (at.place(r) ^ at.side))

    w, r = iota(spread1_ref.shape, 0), iota(spread1_ref.shape, 1)
    spread1_ref[...] = onehot((w_place(w) == at.place(r)) & (w_block(w) == at.local(r)))
    w, r = iota(spread2_ref.shape, 0), iota(spread2_ref.shape, 1)
    spread2_ref[...] = onehot(w_place(w) == (at.block(r) ^ at.chip ^ at.side))

    row, col = iota(keep1_ref.shape, 0), iota(keep1_ref.shape, 1)
    keep1_ref[...] = onehot(at.frame(row) == at.frame(col))
    row, col = iota(keep2_ref.shape, 0), iota(keep2_ref.shape, 1)
    keep2_ref[...] = onehot(
        (at.frame(row) == at.frame(col)) & (at.place(col) == (at.block(row) ^ at.chip))
    )

    row, col = iota(chosen_ref.shape, 0), iota(chosen_ref.shape, 1)
    chosen_ref[...] = onehot(
        (at.block(col) == ((at.side + (row & (bins - 1))) ^ at.chip))
        & (at.place(col) == at.chip)
        & (at.frame(row) == at.frame(col))
    )


def mixing(refs, devices, own, order, selections, keep2):
    valid_ref, pick1_ref, spread1_ref, keep1_ref, pick2_ref, spread2_ref = selections
    per_x = 3 * own + W_ROWS
    factors = jnp.concatenate(
        [piece(refs, per_x, devices, j, 3 * own, W_ROWS) for j in order], 0
    )
    tiles = tiles_of(refs, per_x, devices, own, order)
    picked = [
        mul(pick[...], factors, NT).astype(bf16) * valid_ref[...] for pick in (pick1_ref, pick2_ref)
    ]
    mix1 = mul(picked[0], spread1_ref[...]).astype(bf16) * keep1_ref[...]
    mix2 = mul(picked[1], spread2_ref[...]).astype(bf16) * keep2
    return tiles, mul(mix1, jnp.concatenate(tiles, 1)).astype(bf16), mix2


def near_kernel(
    x0, x1, valid_ref, pick1_ref, spread1_ref, keep1_ref, pick2_ref, spread2_ref, keep2_ref,
    first_ref, mix2_ref, part_ref, own_ref, mark_ref,
):
    own = own_ref.shape[0] // 2
    half, rows = mix2_ref.shape
    devices = rows // own
    selections = (valid_ref, pick1_ref, spread1_ref, keep1_ref, pick2_ref, spread2_ref)
    tiles, first, mix2 = mixing(
        (x0, x1), devices, own, halves_of(devices)[0], selections, keep2_ref[:half, :]
    )
    first_ref[...] = first
    mix2_ref[...] = mix2
    part_ref[...] = mul(mix2[:, :half], first)
    own_ref[:own, :], own_ref[own:, :] = unpacked(*[tile[:own] for tile in tiles])
    mark_ref[...] = jnp.zeros_like(mark_ref)


def mix_kernel(
    x2, x3, x0, x1, first_near_ref, mix2_near_ref, part_ref,
    valid_ref, pick1_ref, spread1_ref, keep1_ref,
    pick2_ref, spread2_ref, keep2_ref,
    sp_ref, back_ref, sp_own_ref, first_far_ref, mark_ref,
):
    own = sp_own_ref.shape[0] // 2
    half, rows = mix2_near_ref.shape
    devices = rows // own
    selections = (valid_ref, pick1_ref, spread1_ref, keep1_ref, pick2_ref, spread2_ref)
    _, first_far, mix2_far = mixing(
        (x0, x1, x2, x3), devices, own, halves_of(devices)[1], selections, keep2_ref[half:, :]
    )
    first = jnp.concatenate([first_near_ref[...], first_far], 0)
    spectral = jnp.concatenate(
        [
            (part_ref[...] + mul(mix2_near_ref[:, half:], first_far)).astype(bf16),
            mul(mix2_far, first).astype(bf16),
        ],
        0,
    )
    back_ref[:half, :] = mix2_near_ref[:, : 2 * own]
    back_ref[half:, :] = mix2_far[:, : 2 * own]
    sp_low, sp_high = unpacked(*cut(spectral))
    sp_own_ref[:own, :], sp_own_ref[own:, :] = sp_low[:own], sp_high[:own]
    first_far_ref[...] = first_far
    sp_ref[:rows, :] = sp_low
    sp_ref[rows:, :] = sp_high
    mark_ref[...] = jnp.zeros_like(mark_ref)


def hidden_kernel(
    sp_ref, w_in_ref, first_near_ref, first_far_ref, chosen_ref,
    hid_ref, slope_ref, spt_ref, first_ref,
):
    own, half = chosen_ref.shape[0], first_near_ref.shape[0]
    first = mul(chosen_ref[:, :half], first_near_ref[...])
    first += mul(chosen_ref[:, half:], first_far_ref[...])
    first_ref[:own, :], first_ref[own:, :] = unpacked(*cut(first.astype(bf16)))
    sp = sp_ref[...]
    gelu_out, slope = gelu_and_slope(mul(sp, w_in_ref[...]))
    hid_ref[...] = gelu_out.astype(bf16)
    slope_ref[...] = slope
    spt_ref[...] = sp.T


def backward_kernel(
    hid_ref, slope_ref, spt_ref, first_ref, back_ref, sp_own_ref, own_ref, d2, d0, d1, d3,
    s_ref, w_in_t_ref, w_out_ref,
    enh_ref, g1_ref, g2_ref, gwi_ref, gwo_ref,
):
    bins, block = g1_ref.shape
    frames, _, channels = s_ref.shape
    half_c = channels // 2
    own = own_ref.shape[0] // 2
    refs = (d0, d1, d2, d3)
    rows = hid_ref.shape[0] // 2
    devices = rows // own
    at = Rows(own, bins, rows)
    order = sum(halves_of(devices), [])
    dm_low, dm_high = unpacked(*tiles_of(refs, 3 * own, devices, own, order))
    parts = 2 * rows // 4
    dm = [half[k : k + parts] for half in (dm_low, dm_high) for k in range(0, rows, parts)]
    dpre, dsp = [], []
    for n, part in enumerate(dm):
        to = slice(n * parts, (n + 1) * parts)
        dpre.append((mul(part, w_out_ref[...]) * slope_ref[to, :]).astype(bf16))
        dsp.append((part.astype(f32) + mul(dpre[n], w_in_t_ref[...])).astype(bf16))
    dpre, dsp = jnp.concatenate(dpre, 0), jnp.concatenate(dsp, 0)
    dsp = dsp[:rows], dsp[rows:]
    gwi_ref[...] = mul(spt_ref[...], dpre)
    gwo_ref[...] = mul(jnp.concatenate([dm_low, dm_high], 0), hid_ref[...], TN)

    sp_own = sp_own_ref[...]
    hidden = jnp.concatenate([hid_ref[:own, :], hid_ref[rows : rows + own, :]], 0)
    mask = (sp_own.astype(f32) + mul(hidden, w_out_ref[...], NT)).astype(bf16).astype(f32)
    spec = s_ref[...].astype(f32).reshape(2 * own, channels)
    spec_re, spec_im = spec[:, :half_c], spec[:, half_c:]
    mask_re, mask_im = mask[:, :half_c], mask[:, half_c:]
    enhanced = jnp.concatenate(
        [spec_re * mask_re - spec_im * mask_im, spec_re * mask_im + spec_im * mask_re], 1
    )
    enh_ref[...] = enhanced.reshape(frames, bins, channels).astype(bf16)

    dsp_low, dsp_high = dsp
    dfirst_low = mul(back_ref[...], dsp_low, TN).astype(bf16)
    dfirst_high = mul(back_ref[...], dsp_high, TN).astype(bf16)

    per_block = at.per_block
    frames_meet = at.frame(iota((own, per_block), 0)) == at.frame(iota((own, per_block), 1))

    def bin_sums(gram):
        parts = jnp.where(frames_meet, gram, 0.0)
        total = sum(parts[n : n + 2 * bins] for n in range(0, own, 2 * bins))
        return total[:bins] + total[bins:]

    gram = mul(own_ref[:own, :], dfirst_low, NT) + mul(own_ref[own:, :], dfirst_high, NT)
    sums = [bin_sums(gram)]
    gram = mul(first_ref[:own, :], dsp_low[:per_block], NT)
    gram += mul(first_ref[own:, :], dsp_high[:per_block], NT)
    sums.append(bin_sums(gram))
    row, col = iota((2 * per_block, 2 * block), 0), iota((2 * per_block, 2 * block), 1)
    place = at.place(row & (per_block - 1))
    take = ((row < per_block) & (place == col)) | (
        (row >= per_block) & (block + (place ^ at.side) == col)
    )
    left, both, chosen = jnp.concatenate(sums, 1), 0.0, onehot(take)
    for _ in range(3):
        part = left.astype(bf16)
        both += mul(part, chosen)
        left -= part.astype(f32)
    g1_ref[...] = both[:, :block]
    g2_ref[...] = both[:, block:]


def whole_rows(features, spectrum, cotangent, w_first, w_second, w_in, w_out):
    frames, bins, channels = features.shape
    block = w_first.shape[1]
    hid = w_in.shape[1]
    devices = lax.axis_size("freq")
    own = frames // 2 * bins
    rows = devices * own
    in_vmem = lambda n: [pl.BlockSpec(memory_space=pltpu.VMEM)] * n
    in_hbm = lambda n: [pl.BlockSpec(memory_space=pltpu.HBM)] * n
    shaped = jax.ShapeDtypeStruct
    params = pltpu.CompilerParams(vmem_limit_bytes=40 * 2**20)
    scale = 1.0 / math.sqrt(frames * devices * bins)
    own_rows, spec_in, w_in_in, w_out_in = pl.pallas_call(
        functools.partial(pack_kernel, scale=scale),
        out_shape=(
            pltpu.VMEM((6 * own + W_ROWS, LANES), bf16),
            pltpu.VMEM((frames, bins, channels), bf16),
            pltpu.VMEM((channels, hid), bf16),
            pltpu.VMEM((channels, hid), bf16),
        ),
        in_specs=in_hbm(7),
        out_specs=tuple(in_vmem(4)),
        scratch_shapes=[
            pltpu.VMEM((frames, bins, channels), bf16),
            pltpu.VMEM((frames, bins, channels), bf16),
            pltpu.VMEM((bins, block), bf16),
            pltpu.VMEM((bins, block), bf16),
            pltpu.SemaphoreType.DMA((7,)),
        ],
        name="pack",
    )(features, spectrum, cotangent, w_first, w_second, w_in, w_out.T)
    w_rows = devices * W_ROWS
    x_own, d_own, w_in_t, *selections = pl.pallas_call(
        functools.partial(prepare_kernel, bins=bins),
        out_shape=tuple(
            pltpu.VMEM(shape, bf16)
            for shape in [
                (3 * own + W_ROWS, LANES),
                (3 * own, LANES),
                (hid, channels),
                (rows // 2, w_rows // 2),
                (rows // 2, LANES),
                (w_rows // 2, rows // 2),
                (rows // 2, rows // 2),
                (rows // 2, LANES),
                (w_rows // 2, rows),
                (rows, rows),
                (own, rows),
            ]
        ),
        in_specs=in_vmem(2),
        out_specs=tuple(in_vmem(11)),
        compiler_params=params,
        cost_estimate=pl.CostEstimate(flops=0, bytes_accessed=2**21, transcendentals=0),
        name="prepare",
    )(own_rows, w_in_in)

    column = [exchanged(own_rows, j) for j in range(devices - 4, 0, -4)]
    x_rows = 3 * own + W_ROWS
    across = exchanged(own_rows, 2)
    x_column = jnp.concatenate([got[:x_rows] for got in column], 0)
    d_column = jnp.concatenate([got[x_rows:] for got in column], 0)
    x2, d2 = exchanged(x_column, 2), exchanged(d_column, 2)
    x0 = jnp.concatenate([x_column, x_own, across[:x_rows]], 0)
    d0 = jnp.concatenate([d_column, d_own, across[x_rows:]], 0)
    x1, d1 = exchanged(x0, 1), exchanged(d0, 1)
    first_near, mix2_near, part, x_rows_own, mark = pl.pallas_call(
        near_kernel,
        out_shape=(
            pltpu.VMEM((rows // 2, 2 * channels), bf16),
            pltpu.VMEM((rows // 2, rows), bf16),
            pltpu.VMEM((rows // 2, 2 * channels), f32),
            pltpu.VMEM((2 * own, channels), bf16),
            pltpu.VMEM((W_ROWS, LANES), bf16),
        ),
        in_specs=in_vmem(9),
        out_specs=tuple(in_vmem(5)),
        compiler_params=params,
        name="near",
    )(x0, x1, *selections[:-1])
    x3 = exchanged(jnp.concatenate([x2, mark], 0), 1)
    spectral, *kept, first_far, mark = pl.pallas_call(
        mix_kernel,
        out_shape=tuple(
            pltpu.VMEM(shape, bf16)
            for shape in [
                (2 * rows, channels),
                (rows, 2 * own),
                (2 * own, channels),
                (rows // 2, 2 * channels),
                (W_ROWS, LANES),
            ]
        ),
        in_specs=in_vmem(14),
        out_specs=tuple(in_vmem(5)),
        compiler_params=params,
        name="mix",
    )(x2, x3, x0, x1, first_near, mix2_near, part, *selections[:-1])
    d3 = exchanged(jnp.concatenate([d2, mark], 0), 1)
    hidden = pl.pallas_call(
        hidden_kernel,
        out_shape=(
            pltpu.VMEM((2 * rows, hid), bf16),
            pltpu.VMEM((2 * rows, hid), f32),
            pltpu.VMEM((channels, 2 * rows), bf16),
            pltpu.VMEM((2 * own, channels), bf16),
        ),
        in_specs=in_vmem(5),
        out_specs=tuple(in_vmem(4)),
        compiler_params=params,
        name="hidden",
    )(spectral, w_in_in, first_near, first_far, selections[-1])

    enhanced, grad_first, grad_second, grad_w_in, grad_w_out = pl.pallas_call(
        backward_kernel,
        out_shape=(
            shaped((frames, bins, channels), bf16),
            shaped((bins, block), f32),
            shaped((bins, block), f32),
            shaped((channels, hid), f32),
            shaped((channels, hid), f32),
        ),
        in_specs=in_vmem(14),
        out_specs=tuple(in_vmem(5)),
        compiler_params=params,
        name="backward",
    )(*hidden, *kept, x_rows_own, d2, d0, d1, d3, spec_in, w_in_t, w_out_in)
    return enhanced, grad_first, grad_second, grad_w_in, grad_w_out.T


def exchanged(value, mask):
    pairs = [(source, source ^ mask) for source in range(lax.axis_size("freq"))]
    return lax.ppermute(value, "freq", pairs)


def on_device(features, spectrum, cotangent, w_first, w_second, w_in, w_out):
    frames, bins, channels = features.shape
    block = w_first.shape[1]
    devices = lax.axis_size("freq")
    gathered_bytes = 2 * 2 * devices * frames * bins * channels
    fits = gathered_bytes <= 4 * 2**20
    shaped = (
        block == 2 * bins
        and devices == 2 * block
        and bins <= W_ROWS
        and 2 * block <= LANES
        and LANES < channels
        and 2 * (channels - LANES) == LANES
        and devices % 4 == 0
    )
    plan = whole_rows if fits and shaped else split_rows
    return plan(features, spectrum, cotangent, w_first, w_second, w_in, w_out)


def solution(mesh):
    placed = (
        P("groups", "freq", None),
        P("groups", "freq", None),
        P("groups", "freq", None),
        P("freq", None),
        P("freq", None),
        P(),
        P(),
    )
    return jax.shard_map(
        on_device,
        mesh=mesh,
        in_specs=placed,
        out_specs=(
            P("groups", "freq", None),
            P("freq", "groups"),
            P("freq", "groups"),
            P("groups", None),
            P("groups", None),
        ),
        check_vma=False,
    )
```

```python
import functools
import math

import jax
import jax.numpy as jnp
from jax import lax
from jax.experimental import pallas as pl
from jax.experimental.pallas import tpu as pltpu
from jax.sharding import PartitionSpec as P

gelu_coef = math.sqrt(2.0 / math.pi)


def swapped(value, axis, distance):
    mask = 2**distance
    pairs = [(source, source ^ mask) for source in range(lax.axis_size(axis))]
    return lax.ppermute(value, axis, pairs)


def gelu_pair(pre_act):
    tanh_arg = gelu_coef * (pre_act + 0.044715 * pre_act * pre_act * pre_act)
    tanh_val = jnp.tanh(tanh_arg)
    gelu_out = 0.5 * pre_act * (1.0 + tanh_val)
    gelu_slope = 0.5 * (1.0 + tanh_val) + 0.5 * pre_act * (
        1.0 - tanh_val * tanh_val
    ) * gelu_coef * (1.0 + 3.0 * 0.044715 * pre_act * pre_act)
    return (gelu_out, gelu_slope)


def spread_back(dfirst_two, features):
    frames, own_bins, channels = features.shape
    block = dfirst_two.shape[0]
    quarter = frames // 4
    devices = 2 * block
    send_back = jnp.broadcast_to(dfirst_two[:, None], (block, 2, 2, quarter, channels)).reshape(
        devices, 2 * quarter * channels
    )
    back_rows = lax.all_to_all(send_back, "freq", split_axis=0, concat_axis=0, tiled=True).reshape(
        block, 2, 2, quarter, channels
    )
    by_quarter_x = features.reshape(2, 2, quarter, own_bins, channels)
    return jnp.einsum(
        "hgtbc,pghtc->bp", by_quarter_x, back_rows, preferred_element_type=jnp.float32
    )


def split_rows(features, spectrum, cotangent, w_first, w_second, w_in, w_out):
    frames, own_bins, channels = features.shape
    block = w_first.shape[1]
    quarter = frames // 4
    half_c = channels // 2
    devices = lax.axis_size("freq")
    parity = lax.axis_index("freq") % 2
    lower_side = parity == 0

    def join_halves(mine, theirs, axis):
        return jnp.where(
            lower_side, jnp.concatenate([mine, theirs], axis), jnp.concatenate([theirs, mine], axis)
        )

    got_second = swapped(w_second, "freq", 0)
    full_second = join_halves(w_second, got_second, 0)
    by_quarter = features.reshape(2, 2, quarter, own_bins, channels)
    partials = jnp.einsum(
        "hgtbc,bp->pghtc", by_quarter, w_first, preferred_element_type=jnp.float32
    )
    partials = partials.reshape(devices, 2 * quarter * channels)
    arrived = lax.all_to_all(partials, "freq", split_axis=0, concat_axis=0, tiled=True)
    first_two = arrived.reshape(block, 2, 2, quarter, channels).sum(axis=1).astype(jnp.bfloat16)
    spectral = jnp.einsum(
        "ahtc,aq->htqc", first_two, full_second, preferred_element_type=jnp.float32
    ).astype(jnp.bfloat16)
    flat_rows = spectral.reshape(-1, channels)
    pre_act = jnp.dot(flat_rows, w_in, preferred_element_type=jnp.float32)
    gelu_out, gelu_slope = gelu_pair(pre_act)
    hidden = gelu_out.astype(jnp.bfloat16)
    spectral_mask = (
        flat_rows.astype(jnp.float32) + jnp.dot(hidden, w_out, preferred_element_type=jnp.float32)
    ).astype(jnp.bfloat16)
    spectral_mask = spectral_mask.reshape(2, quarter, block, channels)
    send_mask = lax.dynamic_slice_in_dim(spectral_mask, (1 - parity) * own_bins, own_bins, 2)
    keep_mask = lax.dynamic_slice_in_dim(spectral_mask, parity * own_bins, own_bins, 2)
    got_mask = swapped(send_mask, "freq", 0)
    full_mask = jnp.where(
        lower_side, jnp.stack([keep_mask, got_mask], 1), jnp.stack([got_mask, keep_mask], 1)
    )
    mask_f = full_mask.reshape(frames, own_bins, channels).astype(jnp.float32)
    spec_f = spectrum.astype(jnp.float32)
    mask_re, mask_im = (mask_f[..., :half_c], mask_f[..., half_c:])
    spec_re, spec_im = (spec_f[..., :half_c], spec_f[..., half_c:])
    enhanced = jnp.concatenate(
        [spec_re * mask_re - spec_im * mask_im, spec_re * mask_im + spec_im * mask_re], -1
    ).astype(jnp.bfloat16)
    loss_scale = jnp.float32(1.0) / jnp.sqrt(jnp.float32(frames * devices * own_bins))
    grad_f = cotangent.astype(jnp.float32) * loss_scale
    grad_re, grad_im = (grad_f[..., :half_c], grad_f[..., half_c:])
    dmask = jnp.concatenate(
        [grad_re * spec_re + grad_im * spec_im, grad_im * spec_re - grad_re * spec_im], -1
    ).astype(jnp.bfloat16)
    dmask = dmask.reshape(2, 2, quarter, own_bins, channels)
    send_dmask = lax.dynamic_index_in_dim(dmask, 1 - parity, 1, keepdims=False)
    keep_dmask = lax.dynamic_index_in_dim(dmask, parity, 1, keepdims=False)
    got_dmask = swapped(send_dmask, "freq", 0)
    dmask_rows = join_halves(keep_dmask, got_dmask, 2).reshape(-1, channels)
    dact = jnp.dot(dmask_rows, w_out.T, preferred_element_type=jnp.float32)
    dpre = (dact * gelu_slope).astype(jnp.bfloat16)
    part_out = jnp.dot(hidden.T, dmask_rows, preferred_element_type=jnp.float32)
    part_in = jnp.dot(flat_rows.T, dpre, preferred_element_type=jnp.float32)
    grad_w_in, grad_w_out = lax.psum((part_in, part_out), "freq")
    dspectral = (
        dmask_rows.astype(jnp.float32) + jnp.dot(dpre, w_in.T, preferred_element_type=jnp.float32)
    ).astype(jnp.bfloat16)
    dspectral = dspectral.reshape(2, quarter, block, channels)
    dfirst_two = jnp.einsum(
        "htqc,aq->ahtc", dspectral, full_second, preferred_element_type=jnp.float32
    ).astype(jnp.bfloat16)
    second_part = jnp.einsum(
        "ahtc,htqc->aq", first_two, dspectral, preferred_element_type=jnp.float32
    )
    second_part = second_part.reshape(2, own_bins, block)
    got_part = swapped(
        lax.dynamic_index_in_dim(second_part, 1 - parity, 0, keepdims=False), "freq", 0
    )
    grad_second = lax.dynamic_index_in_dim(second_part, parity, 0, keepdims=False) + got_part
    grad_first = spread_back(dfirst_two, features)
    return (enhanced, grad_first, grad_second, grad_w_in, grad_w_out)


f32, bf16 = jnp.float32, jnp.bfloat16
NN = (((1,), (0,)), ((), ()))
NT = (((1,), (1,)), ((), ()))
TN = (((0,), (0,)), ((), ()))
LANES = 128
W_ROWS = 16


def mul(a, b, dims=NN):
    return lax.dot_general(a, b, dims, preferred_element_type=f32)


def mul_f32(a, b):
    return lax.dot_general(a, b, NN, precision=lax.Precision.HIGHEST, preferred_element_type=f32)


def iota(shape, dim):
    return lax.broadcasted_iota(jnp.int32, shape, dim)


def onehot(cond):
    return cond.astype(f32).astype(bf16)


def gelu_and_slope(v):
    square = v * v
    tanh_val = jnp.tanh(v * (gelu_coef + (gelu_coef * 0.044715) * square))
    half = 0.5 + 0.5 * tanh_val
    out = v * half
    slope = half + out * (1.0 - half) * (
        2.0 * gelu_coef + (6.0 * gelu_coef * 0.044715) * square
    )
    return out, slope


class Rows:
    def __init__(self, own, bins, rows):
        self.own, self.bins, self.per_block = own, bins, 2 * own
        self.half = rows // (2 * self.per_block)
        me = lax.axis_index("freq")
        self.chip, self.side = me >> 1, (me & 1) * bins

    def local(self, r):
        return r // self.per_block

    def block(self, r):
        k = self.local(r)
        return ((k & (self.half - 1)) << 1) | (k // self.half)

    def place(self, r):
        return ((r // self.own) & 1) * self.bins + (r & (self.bins - 1))

    def frame(self, r):
        return (r // self.bins) & (self.own // self.bins - 1)


def pack_rows(rows):
    half = rows.shape[0] // 2
    low, high = rows[:half], rows[half:]
    rest = jnp.concatenate([low[:, LANES:], high[:, LANES:]], 1)
    return low[:, :LANES], high[:, :LANES], rest


def unpacked(low, high, rest):
    split = rest.shape[1] // 2
    return (
        jnp.concatenate([low, rest[:, :split]], 1),
        jnp.concatenate([high, rest[:, split:]], 1),
    )


def cut(value):
    return value[:, :LANES], value[:, LANES : 2 * LANES], value[:, 2 * LANES :]


def received_from(devices):
    column = [*range(devices - 4, 0, -4)]
    near, far = [*column, 0, 2], [j ^ 2 for j in column]
    return [near, [j ^ 1 for j in near], far, [j ^ 1 for j in far]]


def piece(refs, per_device, devices, j, start, size):
    held = received_from(devices)
    n = next(n for n, part in enumerate(held) if j in part)
    at = held[n].index(j) * per_device[n] + start
    return refs[n][at : at + size, :]


def halves_of(devices):
    return [[j for j in range(devices) if j & 2 == bit] for bit in (0, 2)]


def tiles_of(refs, per_device, devices, own, order):
    return [
        jnp.concatenate([piece(refs, per_device, devices, j, t * own, own) for j in order], 0)
        for t in range(3)
    ]


def pack_kernel(
    x_hbm, s_hbm, c_hbm, w1_hbm, w2_hbm, w_in_hbm, w_out_hbm,
    out_ref, s_ref, w_in_ref, w_out_ref,
    x_ref, c_ref, w1_ref, w2_ref, sems, *, scale,
):
    copies = [
        pltpu.make_async_copy(src, dst, sems.at[n])
        for n, (src, dst) in enumerate(
            [
                (x_hbm, x_ref),
                (w1_hbm, w1_ref),
                (w2_hbm, w2_ref),
                (s_hbm, s_ref),
                (c_hbm, c_ref),
                (w_in_hbm, w_in_ref),
                (w_out_hbm, w_out_ref),
            ]
        )
    ]
    for copy in copies:
        copy.start()
    for copy in copies[:3]:
        copy.wait()
    frames, bins, channels = x_ref.shape
    rows = frames * bins
    half = rows // 2
    half_c = channels // 2
    block = w1_ref.shape[1]

    for t, part in enumerate(pack_rows(x_ref[...].astype(f32).reshape(rows, channels))):
        out_ref[t * half : (t + 1) * half, :] = part.astype(bf16)
    weights = jnp.concatenate([w1_ref[...].astype(f32), w2_ref[...].astype(f32)], 1)
    weights = jnp.concatenate([weights, jnp.zeros((bins, LANES - 2 * block), f32)], 1)
    weights = jnp.concatenate([weights, jnp.zeros((W_ROWS - bins, LANES), f32)], 0)
    start = 3 * half + W_ROWS
    out_ref[3 * half : start, :] = weights.astype(bf16)

    for copy in copies[3:5]:
        copy.wait()
    spec = s_ref[...].astype(f32).reshape(rows, channels)
    grad = c_ref[...].astype(f32).reshape(rows, channels) * scale
    spec_re, spec_im = spec[:, :half_c], spec[:, half_c:]
    grad_re, grad_im = grad[:, :half_c], grad[:, half_c:]
    dmask = jnp.concatenate(
        [grad_re * spec_re + grad_im * spec_im, grad_im * spec_re - grad_re * spec_im], 1
    )
    for t, part in enumerate(pack_rows(dmask)):
        out_ref[start + t * half : start + (t + 1) * half, :] = part.astype(bf16)
    for copy in copies[5:]:
        copy.wait()


def prepare_kernel(
    own_ref, w_in_ref, x_ref, d_ref, w_in_t_ref, valid_ref, pick1_ref, spread1_ref, keep1_ref,
    pick2_ref, spread2_ref, keep2_ref, valid_far_ref, spread1_far_ref, spread2_far_ref, chosen_ref,
    *, bins,
):
    w_in_t_ref[...] = w_in_ref[...].T
    x_ref[...] = own_ref[: x_ref.shape[0], :]
    d_ref[...] = own_ref[x_ref.shape[0] :, :]
    own, rows = chosen_ref.shape
    block = 2 * bins
    at = Rows(own, bins, rows)

    def w_place(r):
        return ((r // W_ROWS) & 1) * bins + (r & (W_ROWS - 1))

    def w_block(r):
        return r // (2 * W_ROWS)

    r, w = iota(valid_ref.shape, 0), iota(valid_ref.shape, 1)
    valid_ref[...] = onehot(((w & (W_ROWS - 1)) < bins) & (w_block(w) == at.local(r)))

    r, lane = iota(pick1_ref.shape, 0), iota(pick1_ref.shape, 1)
    pick1_ref[...] = onehot(lane == at.place(r))
    pick2_ref[...] = onehot(lane == block + (at.place(r) ^ at.side))

    w, r = iota(spread1_ref.shape, 0), iota(spread1_ref.shape, 1)
    spread1_ref[...] = onehot((w_place(w) == at.place(r)) & (w_block(w) == at.local(r)))
    w, r = iota(spread2_ref.shape, 0), iota(spread2_ref.shape, 1)
    spread2_ref[...] = onehot(w_place(w) == (at.block(r) ^ at.chip ^ at.side))

    row, col = iota(keep1_ref.shape, 0), iota(keep1_ref.shape, 1)
    keep1_ref[...] = onehot(at.frame(row) == at.frame(col))
    row, col = iota(keep2_ref.shape, 0), iota(keep2_ref.shape, 1)
    keep2_ref[...] = onehot(
        (at.frame(row) == at.frame(col)) & (at.place(col) == (at.block(row) ^ at.chip))
    )

    def far_place(r):
        return (r // W_ROWS) * bins + (r & (bins - 1))

    def far_local(r):
        return W_ROWS // bins - 1 - (r & (W_ROWS - 1)) // bins

    r, w = iota(valid_far_ref.shape, 0), iota(valid_far_ref.shape, 1)
    valid_far_ref[...] = onehot(far_local(w) == at.local(r))
    w, r = iota(spread1_far_ref.shape, 0), iota(spread1_far_ref.shape, 1)
    spread1_far_ref[...] = onehot((far_place(w) == at.place(r)) & (far_local(w) == at.local(r)))
    w, r = iota(spread2_far_ref.shape, 0), iota(spread2_far_ref.shape, 1)
    spread2_far_ref[...] = onehot(far_place(w) == (at.block(r) ^ at.chip ^ at.side))

    row, col = iota(chosen_ref.shape, 0), iota(chosen_ref.shape, 1)
    chosen_ref[...] = onehot(
        (at.block(col) == ((at.side + (row & (bins - 1))) ^ at.chip))
        & (at.place(col) == at.chip)
        & (at.frame(row) == at.frame(col))
    )


def x_rows_of(own):
    return (3 * own + W_ROWS,) * 2 + (3 * own,) * 2


def mixing(refs, devices, own, order, factors, selections, keep2):
    valid_ref, pick1_ref, spread1_ref, keep1_ref, pick2_ref, spread2_ref = selections
    tiles = tiles_of(refs, x_rows_of(own), devices, own, order)
    picked = [
        mul(pick[...], factors, NT).astype(bf16) * valid_ref[...] for pick in (pick1_ref, pick2_ref)
    ]
    mix1 = mul(picked[0], spread1_ref[...]).astype(bf16) * keep1_ref[...]
    mix2 = mul(picked[1], spread2_ref[...]).astype(bf16) * keep2
    return tiles, mul(mix1, jnp.concatenate(tiles, 1)).astype(bf16), mix2


def near_kernel(
    x0, x1, valid_ref, pick1_ref, spread1_ref, keep1_ref, pick2_ref, spread2_ref, keep2_ref,
    first_ref, mix2_ref, part_ref, own_ref, mark_ref,
):
    own = own_ref.shape[0] // 2
    half, rows = mix2_ref.shape
    devices = rows // own
    selections = (valid_ref, pick1_ref, spread1_ref, keep1_ref, pick2_ref, spread2_ref)
    order = halves_of(devices)[0]
    factors = [piece((x0, x1), x_rows_of(own), devices, j, 3 * own, W_ROWS) for j in order]
    tiles, first, mix2 = mixing(
        (x0, x1), devices, own, order, jnp.concatenate(factors, 0), selections, keep2_ref[:half, :]
    )
    first_ref[...] = first
    mix2_ref[...] = mix2
    part_ref[...] = mul(mix2[:, :half], first)
    own_ref[:own, :], own_ref[own:, :] = unpacked(*[tile[:own] for tile in tiles])
    mark_ref[...] = jnp.zeros_like(mark_ref)


def mix_kernel(
    x2, x3, x0, x1, first_near_ref, mix2_near_ref, part_ref,
    valid_ref, pick1_ref, spread1_ref, keep1_ref,
    pick2_ref, spread2_ref, keep2_ref,
    sp_ref, back_ref, sp_own_ref, first_far_ref, mark_ref,
):
    own = sp_own_ref.shape[0] // 2
    half, rows = mix2_near_ref.shape
    devices = rows // own
    selections = (valid_ref, pick1_ref, spread1_ref, keep1_ref, pick2_ref, spread2_ref)
    at_end = (devices // 4 - 1) * 3 * own
    factors = jnp.concatenate([ref[at_end : at_end + W_ROWS, :] for ref in (x2, x3)], 0)
    _, first_far, mix2_far = mixing(
        (x0, x1, x2, x3), devices, own, halves_of(devices)[1], factors, selections, keep2_ref[half:, :]
    )
    first = jnp.concatenate([first_near_ref[...], first_far], 0)
    spectral = jnp.concatenate(
        [
            (part_ref[...] + mul(mix2_near_ref[:, half:], first_far)).astype(bf16),
            mul(mix2_far, first).astype(bf16),
        ],
        0,
    )
    back_ref[:half, :] = mix2_near_ref[:, : 2 * own]
    back_ref[half:, :] = mix2_far[:, : 2 * own]
    sp_low, sp_high = unpacked(*cut(spectral))
    sp_own_ref[:own, :], sp_own_ref[own:, :] = sp_low[:own], sp_high[:own]
    first_far_ref[...] = first_far
    sp_ref[:rows, :] = sp_low
    sp_ref[rows:, :] = sp_high
    mark_ref[...] = jnp.zeros_like(mark_ref)


def hidden_kernel(
    sp_ref, w_in_ref, first_near_ref, first_far_ref, chosen_ref,
    hid_ref, slope_ref, spt_ref, first_ref,
):
    own, half = chosen_ref.shape[0], first_near_ref.shape[0]
    first = mul(chosen_ref[:, :half], first_near_ref[...])
    first += mul(chosen_ref[:, half:], first_far_ref[...])
    first_ref[:own, :], first_ref[own:, :] = unpacked(*cut(first.astype(bf16)))
    sp = sp_ref[...]
    gelu_out, slope = gelu_and_slope(mul(sp, w_in_ref[...]))
    hid_ref[...] = gelu_out.astype(bf16)
    slope_ref[...] = slope
    spt_ref[...] = sp.T


def backward_kernel(
    hid_ref, slope_ref, spt_ref, first_ref, back_ref, sp_own_ref, own_ref, d2, d0, d1, d3,
    s_ref, w_in_t_ref, w_out_ref,
    enh_ref, g1_ref, g2_ref, gwi_ref, gwo_ref,
):
    bins, block = g1_ref.shape
    frames, _, channels = s_ref.shape
    half_c = channels // 2
    own = own_ref.shape[0] // 2
    refs = (d0, d1, d2, d3)
    rows = hid_ref.shape[0] // 2
    devices = rows // own
    at = Rows(own, bins, rows)
    order = sum(halves_of(devices), [])
    dm_low, dm_high = unpacked(*tiles_of(refs, (3 * own,) * 4, devices, own, order))
    parts = 2 * rows // 4
    dm = [half[k : k + parts] for half in (dm_low, dm_high) for k in range(0, rows, parts)]
    dpre, dsp = [], []
    for n, part in enumerate(dm):
        to = slice(n * parts, (n + 1) * parts)
        dpre.append((mul(part, w_out_ref[...]) * slope_ref[to, :]).astype(bf16))
        dsp.append((part.astype(f32) + mul(dpre[n], w_in_t_ref[...])).astype(bf16))
    dpre, dsp = jnp.concatenate(dpre, 0), jnp.concatenate(dsp, 0)
    dsp = dsp[:rows], dsp[rows:]
    gwi_ref[...] = mul(spt_ref[...], dpre)
    gwo_ref[...] = mul(jnp.concatenate([dm_low, dm_high], 0), hid_ref[...], TN)

    sp_own = sp_own_ref[...]
    hidden = jnp.concatenate([hid_ref[:own, :], hid_ref[rows : rows + own, :]], 0)
    mask = (sp_own.astype(f32) + mul(hidden, w_out_ref[...], NT)).astype(bf16).astype(f32)
    spec = s_ref[...].astype(f32).reshape(2 * own, channels)
    spec_re, spec_im = spec[:, :half_c], spec[:, half_c:]
    mask_re, mask_im = mask[:, :half_c], mask[:, half_c:]
    enhanced = jnp.concatenate(
        [spec_re * mask_re - spec_im * mask_im, spec_re * mask_im + spec_im * mask_re], 1
    )
    enh_ref[...] = enhanced.reshape(frames, bins, channels).astype(bf16)

    dsp_low, dsp_high = dsp
    dfirst_low = mul(back_ref[...], dsp_low, TN).astype(bf16)
    dfirst_high = mul(back_ref[...], dsp_high, TN).astype(bf16)

    per_block = at.per_block
    frames_meet = at.frame(iota((own, per_block), 0)) == at.frame(iota((own, per_block), 1))

    def bin_sums(gram):
        parts = jnp.where(frames_meet, gram, 0.0)
        total = sum(parts[n : n + 2 * bins] for n in range(0, own, 2 * bins))
        return total[:bins] + total[bins:]

    gram = mul(own_ref[:own, :], dfirst_low, NT) + mul(own_ref[own:, :], dfirst_high, NT)
    sums = [bin_sums(gram)]
    gram = mul(first_ref[:own, :], dsp_low[:per_block], NT)
    gram += mul(first_ref[own:, :], dsp_high[:per_block], NT)
    sums.append(bin_sums(gram))
    row, col = iota((2 * per_block, 2 * block), 0), iota((2 * per_block, 2 * block), 1)
    place = at.place(row & (per_block - 1))
    take = ((row < per_block) & (place == col)) | (
        (row >= per_block) & (block + (place ^ at.side) == col)
    )
    left, both, chosen = jnp.concatenate(sums, 1), 0.0, onehot(take)
    for _ in range(3):
        part = left.astype(bf16)
        both += mul(part, chosen)
        left -= part.astype(f32)
    g1_ref[...] = both[:, :block]
    g2_ref[...] = both[:, block:]


def whole_rows(features, spectrum, cotangent, w_first, w_second, w_in, w_out):
    frames, bins, channels = features.shape
    block = w_first.shape[1]
    hid = w_in.shape[1]
    devices = lax.axis_size("freq")
    own = frames // 2 * bins
    rows = devices * own
    in_vmem = lambda n: [pl.BlockSpec(memory_space=pltpu.VMEM)] * n
    in_hbm = lambda n: [pl.BlockSpec(memory_space=pltpu.HBM)] * n
    shaped = jax.ShapeDtypeStruct
    params = pltpu.CompilerParams(vmem_limit_bytes=40 * 2**20)
    scale = 1.0 / math.sqrt(frames * devices * bins)
    own_rows, spec_in, w_in_in, w_out_in = pl.pallas_call(
        functools.partial(pack_kernel, scale=scale),
        out_shape=(
            pltpu.VMEM((6 * own + W_ROWS, LANES), bf16),
            pltpu.VMEM((frames, bins, channels), bf16),
            pltpu.VMEM((channels, hid), bf16),
            pltpu.VMEM((channels, hid), bf16),
        ),
        in_specs=in_hbm(7),
        out_specs=tuple(in_vmem(4)),
        scratch_shapes=[
            pltpu.VMEM((frames, bins, channels), bf16),
            pltpu.VMEM((frames, bins, channels), bf16),
            pltpu.VMEM((bins, block), bf16),
            pltpu.VMEM((bins, block), bf16),
            pltpu.SemaphoreType.DMA((7,)),
        ],
        name="pack",
    )(features, spectrum, cotangent, w_first, w_second, w_in, w_out.T)
    w_rows = devices * W_ROWS
    x_own, d_own, w_in_t, *selections = pl.pallas_call(
        functools.partial(prepare_kernel, bins=bins),
        out_shape=tuple(
            pltpu.VMEM(shape, bf16)
            for shape in [
                (3 * own + W_ROWS, LANES),
                (3 * own, LANES),
                (hid, channels),
                (rows // 2, w_rows // 2),
                (rows // 2, LANES),
                (w_rows // 2, rows // 2),
                (rows // 2, rows // 2),
                (rows // 2, LANES),
                (w_rows // 2, rows),
                (rows, rows),
                (rows // 2, 2 * W_ROWS),
                (2 * W_ROWS, rows // 2),
                (2 * W_ROWS, rows),
                (own, rows),
            ]
        ),
        in_specs=in_vmem(2),
        out_specs=tuple(in_vmem(14)),
        compiler_params=params,
        cost_estimate=pl.CostEstimate(flops=0, bytes_accessed=2**21, transcendentals=0),
        name="prepare",
    )(own_rows, w_in_in)

    column = [exchanged(own_rows, j) for j in range(devices - 4, 0, -4)]
    x_rows = 3 * own + W_ROWS
    across = exchanged(own_rows, 2)
    sent = [*column, own_rows]
    x_column = jnp.concatenate(
        [got[: 3 * own] for got in column]
        + [got[3 * own : 3 * own + bins] for got in sent],
        0,
    )
    d_column = jnp.concatenate([got[x_rows:] for got in column], 0)
    x2, d2 = exchanged(x_column, 2), exchanged(d_column, 2)
    x0 = jnp.concatenate([*[got[:x_rows] for got in column], x_own, across[:x_rows]], 0)
    d0 = jnp.concatenate([d_column, d_own, across[x_rows:]], 0)
    x1, d1 = exchanged(x0, 1), exchanged(d0, 1)
    first_near, mix2_near, part, x_rows_own, mark = pl.pallas_call(
        near_kernel,
        out_shape=(
            pltpu.VMEM((rows // 2, 2 * channels), bf16),
            pltpu.VMEM((rows // 2, rows), bf16),
            pltpu.VMEM((rows // 2, 2 * channels), f32),
            pltpu.VMEM((2 * own, channels), bf16),
            pltpu.VMEM((W_ROWS, LANES), bf16),
        ),
        in_specs=in_vmem(9),
        out_specs=tuple(in_vmem(5)),
        compiler_params=params,
        name="near",
    )(x0, x1, *selections[:7])
    x3 = exchanged(jnp.concatenate([x2, mark], 0), 1)
    pick1, keep1, pick2, keep2 = (selections[n] for n in (1, 3, 4, 6))
    valid_far, spread1_far, spread2_far = selections[7:10]
    spectral, *kept, first_far, mark = pl.pallas_call(
        mix_kernel,
        out_shape=tuple(
            pltpu.VMEM(shape, bf16)
            for shape in [
                (2 * rows, channels),
                (rows, 2 * own),
                (2 * own, channels),
                (rows // 2, 2 * channels),
                (W_ROWS, LANES),
            ]
        ),
        in_specs=in_vmem(14),
        out_specs=tuple(in_vmem(5)),
        compiler_params=params,
        name="mix",
    )(
        x2, x3, x0, x1, first_near, mix2_near, part,
        valid_far, pick1, spread1_far, keep1, pick2, spread2_far, keep2,
    )
    d3 = exchanged(jnp.concatenate([d2, mark], 0), 1)
    hidden = pl.pallas_call(
        hidden_kernel,
        out_shape=(
            pltpu.VMEM((2 * rows, hid), bf16),
            pltpu.VMEM((2 * rows, hid), f32),
            pltpu.VMEM((channels, 2 * rows), bf16),
            pltpu.VMEM((2 * own, channels), bf16),
        ),
        in_specs=in_vmem(5),
        out_specs=tuple(in_vmem(4)),
        compiler_params=params,
        name="hidden",
    )(spectral, w_in_in, first_near, first_far, selections[-1])

    enhanced, grad_first, grad_second, grad_w_in, grad_w_out = pl.pallas_call(
        backward_kernel,
        out_shape=(
            shaped((frames, bins, channels), bf16),
            shaped((bins, block), f32),
            shaped((bins, block), f32),
            shaped((channels, hid), f32),
            shaped((channels, hid), f32),
        ),
        in_specs=in_vmem(14),
        out_specs=tuple(in_vmem(5)),
        compiler_params=params,
        name="backward",
    )(*hidden, *kept, x_rows_own, d2, d0, d1, d3, spec_in, w_in_t, w_out_in)
    return enhanced, grad_first, grad_second, grad_w_in, grad_w_out.T


def exchanged(value, mask):
    pairs = [(source, source ^ mask) for source in range(lax.axis_size("freq"))]
    return lax.ppermute(value, "freq", pairs)


def on_device(features, spectrum, cotangent, w_first, w_second, w_in, w_out):
    frames, bins, channels = features.shape
    block = w_first.shape[1]
    devices = lax.axis_size("freq")
    gathered_bytes = 2 * 2 * devices * frames * bins * channels
    fits = gathered_bytes <= 4 * 2**20
    shaped = (
        block == 2 * bins
        and devices == 2 * block
        and bins <= W_ROWS
        and 2 * block <= LANES
        and LANES < channels
        and 2 * (channels - LANES) == LANES
        and devices % 4 == 0
        and devices // 4 * bins == W_ROWS
    )
    plan = whole_rows if fits and shaped else split_rows
    return plan(features, spectrum, cotangent, w_first, w_second, w_in, w_out)


def solution(mesh):
    placed = (
        P("groups", "freq", None),
        P("groups", "freq", None),
        P("groups", "freq", None),
        P("freq", None),
        P("freq", None),
        P(),
        P(),
    )
    return jax.shard_map(
        on_device,
        mesh=mesh,
        in_specs=placed,
        out_specs=(
            P("groups", "freq", None),
            P("freq", "groups"),
            P("freq", "groups"),
            P("groups", None),
            P("groups", None),
        ),
        check_vma=False,
    )
```

```python
import functools
import math

import jax
import jax.numpy as jnp
from jax import lax
from jax.experimental import pallas as pl
from jax.experimental.pallas import tpu as pltpu
from jax.sharding import PartitionSpec as P

gelu_coef = math.sqrt(2.0 / math.pi)


def swapped(value, axis, distance):
    mask = 2**distance
    pairs = [(source, source ^ mask) for source in range(lax.axis_size(axis))]
    return lax.ppermute(value, axis, pairs)


def gelu_pair(pre_act):
    tanh_arg = gelu_coef * (pre_act + 0.044715 * pre_act * pre_act * pre_act)
    tanh_val = jnp.tanh(tanh_arg)
    gelu_out = 0.5 * pre_act * (1.0 + tanh_val)
    gelu_slope = 0.5 * (1.0 + tanh_val) + 0.5 * pre_act * (
        1.0 - tanh_val * tanh_val
    ) * gelu_coef * (1.0 + 3.0 * 0.044715 * pre_act * pre_act)
    return (gelu_out, gelu_slope)


def spread_back(dfirst_two, features):
    frames, own_bins, channels = features.shape
    block = dfirst_two.shape[0]
    quarter = frames // 4
    devices = 2 * block
    send_back = jnp.broadcast_to(dfirst_two[:, None], (block, 2, 2, quarter, channels)).reshape(
        devices, 2 * quarter * channels
    )
    back_rows = lax.all_to_all(send_back, "freq", split_axis=0, concat_axis=0, tiled=True).reshape(
        block, 2, 2, quarter, channels
    )
    by_quarter_x = features.reshape(2, 2, quarter, own_bins, channels)
    return jnp.einsum(
        "hgtbc,pghtc->bp", by_quarter_x, back_rows, preferred_element_type=jnp.float32
    )


def split_rows(features, spectrum, cotangent, w_first, w_second, w_in, w_out):
    frames, own_bins, channels = features.shape
    block = w_first.shape[1]
    quarter = frames // 4
    half_c = channels // 2
    devices = lax.axis_size("freq")
    parity = lax.axis_index("freq") % 2
    lower_side = parity == 0

    def join_halves(mine, theirs, axis):
        return jnp.where(
            lower_side, jnp.concatenate([mine, theirs], axis), jnp.concatenate([theirs, mine], axis)
        )

    got_second = swapped(w_second, "freq", 0)
    full_second = join_halves(w_second, got_second, 0)
    by_quarter = features.reshape(2, 2, quarter, own_bins, channels)
    partials = jnp.einsum(
        "hgtbc,bp->pghtc", by_quarter, w_first, preferred_element_type=jnp.float32
    )
    partials = partials.reshape(devices, 2 * quarter * channels)
    arrived = lax.all_to_all(partials, "freq", split_axis=0, concat_axis=0, tiled=True)
    first_two = arrived.reshape(block, 2, 2, quarter, channels).sum(axis=1).astype(jnp.bfloat16)
    spectral = jnp.einsum(
        "ahtc,aq->htqc", first_two, full_second, preferred_element_type=jnp.float32
    ).astype(jnp.bfloat16)
    flat_rows = spectral.reshape(-1, channels)
    pre_act = jnp.dot(flat_rows, w_in, preferred_element_type=jnp.float32)
    gelu_out, gelu_slope = gelu_pair(pre_act)
    hidden = gelu_out.astype(jnp.bfloat16)
    spectral_mask = (
        flat_rows.astype(jnp.float32) + jnp.dot(hidden, w_out, preferred_element_type=jnp.float32)
    ).astype(jnp.bfloat16)
    spectral_mask = spectral_mask.reshape(2, quarter, block, channels)
    send_mask = lax.dynamic_slice_in_dim(spectral_mask, (1 - parity) * own_bins, own_bins, 2)
    keep_mask = lax.dynamic_slice_in_dim(spectral_mask, parity * own_bins, own_bins, 2)
    got_mask = swapped(send_mask, "freq", 0)
    full_mask = jnp.where(
        lower_side, jnp.stack([keep_mask, got_mask], 1), jnp.stack([got_mask, keep_mask], 1)
    )
    mask_f = full_mask.reshape(frames, own_bins, channels).astype(jnp.float32)
    spec_f = spectrum.astype(jnp.float32)
    mask_re, mask_im = (mask_f[..., :half_c], mask_f[..., half_c:])
    spec_re, spec_im = (spec_f[..., :half_c], spec_f[..., half_c:])
    enhanced = jnp.concatenate(
        [spec_re * mask_re - spec_im * mask_im, spec_re * mask_im + spec_im * mask_re], -1
    ).astype(jnp.bfloat16)
    loss_scale = jnp.float32(1.0) / jnp.sqrt(jnp.float32(frames * devices * own_bins))
    grad_f = cotangent.astype(jnp.float32) * loss_scale
    grad_re, grad_im = (grad_f[..., :half_c], grad_f[..., half_c:])
    dmask = jnp.concatenate(
        [grad_re * spec_re + grad_im * spec_im, grad_im * spec_re - grad_re * spec_im], -1
    ).astype(jnp.bfloat16)
    dmask = dmask.reshape(2, 2, quarter, own_bins, channels)
    send_dmask = lax.dynamic_index_in_dim(dmask, 1 - parity, 1, keepdims=False)
    keep_dmask = lax.dynamic_index_in_dim(dmask, parity, 1, keepdims=False)
    got_dmask = swapped(send_dmask, "freq", 0)
    dmask_rows = join_halves(keep_dmask, got_dmask, 2).reshape(-1, channels)
    dact = jnp.dot(dmask_rows, w_out.T, preferred_element_type=jnp.float32)
    dpre = (dact * gelu_slope).astype(jnp.bfloat16)
    part_out = jnp.dot(hidden.T, dmask_rows, preferred_element_type=jnp.float32)
    part_in = jnp.dot(flat_rows.T, dpre, preferred_element_type=jnp.float32)
    grad_w_in, grad_w_out = lax.psum((part_in, part_out), "freq")
    dspectral = (
        dmask_rows.astype(jnp.float32) + jnp.dot(dpre, w_in.T, preferred_element_type=jnp.float32)
    ).astype(jnp.bfloat16)
    dspectral = dspectral.reshape(2, quarter, block, channels)
    dfirst_two = jnp.einsum(
        "htqc,aq->ahtc", dspectral, full_second, preferred_element_type=jnp.float32
    ).astype(jnp.bfloat16)
    second_part = jnp.einsum(
        "ahtc,htqc->aq", first_two, dspectral, preferred_element_type=jnp.float32
    )
    second_part = second_part.reshape(2, own_bins, block)
    got_part = swapped(
        lax.dynamic_index_in_dim(second_part, 1 - parity, 0, keepdims=False), "freq", 0
    )
    grad_second = lax.dynamic_index_in_dim(second_part, parity, 0, keepdims=False) + got_part
    grad_first = spread_back(dfirst_two, features)
    return (enhanced, grad_first, grad_second, grad_w_in, grad_w_out)


f32, bf16 = jnp.float32, jnp.bfloat16
NN = (((1,), (0,)), ((), ()))
NT = (((1,), (1,)), ((), ()))
TN = (((0,), (0,)), ((), ()))
LANES = 128
W_ROWS = 16


def mul(a, b, dims=NN):
    return lax.dot_general(a, b, dims, preferred_element_type=f32)


def mul_f32(a, b):
    return lax.dot_general(a, b, NN, precision=lax.Precision.HIGHEST, preferred_element_type=f32)


def iota(shape, dim):
    return lax.broadcasted_iota(jnp.int32, shape, dim)


def onehot(cond):
    return cond.astype(f32).astype(bf16)


def gelu_and_slope(v):
    square = v * v
    tanh_val = jnp.tanh(v * (gelu_coef + (gelu_coef * 0.044715) * square))
    half = 0.5 + 0.5 * tanh_val
    out = v * half
    slope = half + out * (1.0 - half) * (
        2.0 * gelu_coef + (6.0 * gelu_coef * 0.044715) * square
    )
    return out, slope


class Rows:
    def __init__(self, own, bins, rows):
        self.own, self.bins, self.per_block = own, bins, 2 * own
        self.half = rows // (2 * self.per_block)
        me = lax.axis_index("freq")
        self.chip, self.side = me >> 1, (me & 1) * bins

    def local(self, r):
        return r // self.per_block

    def block(self, r):
        k = self.local(r)
        return ((k & (self.half - 1)) << 1) | (k // self.half)

    def place(self, r):
        return ((r // self.own) & 1) * self.bins + (r & (self.bins - 1))

    def frame(self, r):
        return (r // self.bins) & (self.own // self.bins - 1)


def pack_rows(rows):
    half = rows.shape[0] // 2
    low, high = rows[:half], rows[half:]
    rest = jnp.concatenate([low[:, LANES:], high[:, LANES:]], 1)
    return low[:, :LANES], high[:, :LANES], rest


def unpacked(low, high, rest):
    split = rest.shape[1] // 2
    return (
        jnp.concatenate([low, rest[:, :split]], 1),
        jnp.concatenate([high, rest[:, split:]], 1),
    )


def cut(value):
    return value[:, :LANES], value[:, LANES : 2 * LANES], value[:, 2 * LANES :]


def received_from(devices):
    column = [*range(devices - 4, 0, -4)]
    near, far = [*column, 0, 2], [j ^ 2 for j in column]
    return [near, [j ^ 1 for j in near], far, [j ^ 1 for j in far]]


def piece(refs, per_device, devices, j, start, size):
    held = received_from(devices)
    n = next(n for n, part in enumerate(held) if j in part)
    at = held[n].index(j) * per_device[n] + start
    return refs[n][at : at + size, :]


def halves_of(devices):
    return [[j for j in range(devices) if j & 2 == bit] for bit in (0, 2)]


def tiles_of(refs, per_device, devices, own, order):
    return [
        jnp.concatenate([piece(refs, per_device, devices, j, t * own, own) for j in order], 0)
        for t in range(3)
    ]


def pack_kernel(
    x_hbm, s_hbm, c_hbm, w1_hbm, w2_hbm, w_in_hbm, w_out_hbm,
    out_ref, s_ref, w_in_ref, w_out_ref,
    x_ref, c_ref, w1_ref, w2_ref, sems, *, scale,
):
    copies = [
        pltpu.make_async_copy(src, dst, sems.at[n])
        for n, (src, dst) in enumerate(
            [
                (x_hbm, x_ref),
                (w1_hbm, w1_ref),
                (w2_hbm, w2_ref),
                (s_hbm, s_ref),
                (c_hbm, c_ref),
                (w_in_hbm, w_in_ref),
                (w_out_hbm, w_out_ref),
            ]
        )
    ]
    for copy in copies:
        copy.start()
    for copy in copies[:3]:
        copy.wait()
    frames, bins, channels = x_ref.shape
    rows = frames * bins
    half = rows // 2
    half_c = channels // 2
    block = w1_ref.shape[1]

    for t, part in enumerate(pack_rows(x_ref[...].astype(f32).reshape(rows, channels))):
        out_ref[t * half : (t + 1) * half, :] = part.astype(bf16)
    weights = jnp.concatenate([w1_ref[...].astype(f32), w2_ref[...].astype(f32)], 1)
    weights = jnp.concatenate([weights, jnp.zeros((bins, LANES - 2 * block), f32)], 1)
    weights = jnp.concatenate([weights, jnp.zeros((W_ROWS - bins, LANES), f32)], 0)
    start = 3 * half + W_ROWS
    out_ref[3 * half : start, :] = weights.astype(bf16)

    for copy in copies[3:5]:
        copy.wait()
    spec = s_ref[...].astype(f32).reshape(rows, channels)
    grad = c_ref[...].astype(f32).reshape(rows, channels) * scale
    spec_re, spec_im = spec[:, :half_c], spec[:, half_c:]
    grad_re, grad_im = grad[:, :half_c], grad[:, half_c:]
    dmask = jnp.concatenate(
        [grad_re * spec_re + grad_im * spec_im, grad_im * spec_re - grad_re * spec_im], 1
    )
    for t, part in enumerate(pack_rows(dmask)):
        out_ref[start + t * half : start + (t + 1) * half, :] = part.astype(bf16)
    for copy in copies[5:]:
        copy.wait()


def prepare_kernel(
    own_ref, w_in_ref, x_ref, d_ref, w_in_t_ref, valid_ref, pick1_ref, spread1_ref, keep1_ref,
    pick2_ref, spread2_ref, keep2_ref, valid_far_ref, spread1_far_ref, spread2_far_ref, chosen_ref,
    *, bins,
):
    w_in_t_ref[...] = w_in_ref[...].T
    x_ref[...] = own_ref[: x_ref.shape[0], :]
    d_ref[...] = own_ref[x_ref.shape[0] :, :]
    own, rows = chosen_ref.shape
    block = 2 * bins
    at = Rows(own, bins, rows)

    def w_place(r):
        return ((r // W_ROWS) & 1) * bins + (r & (W_ROWS - 1))

    def w_block(r):
        return r // (2 * W_ROWS)

    r, w = iota(valid_ref.shape, 0), iota(valid_ref.shape, 1)
    valid_ref[...] = onehot(((w & (W_ROWS - 1)) < bins) & (w_block(w) == at.local(r)))

    r, lane = iota(pick1_ref.shape, 0), iota(pick1_ref.shape, 1)
    pick1_ref[...] = onehot(lane == at.place(r))
    pick2_ref[...] = onehot(lane == block + (at.place(r) ^ at.side))

    w, r = iota(spread1_ref.shape, 0), iota(spread1_ref.shape, 1)
    spread1_ref[...] = onehot((w_place(w) == at.place(r)) & (w_block(w) == at.local(r)))
    w, r = iota(spread2_ref.shape, 0), iota(spread2_ref.shape, 1)
    spread2_ref[...] = onehot(w_place(w) == (at.block(r) ^ at.chip ^ at.side))

    row, col = iota(keep1_ref.shape, 0), iota(keep1_ref.shape, 1)
    keep1_ref[...] = onehot(at.frame(row) == at.frame(col))
    row, col = iota(keep2_ref.shape, 0), iota(keep2_ref.shape, 1)
    keep2_ref[...] = onehot(
        (at.frame(row) == at.frame(col)) & (at.place(col) == (at.block(row) ^ at.chip))
    )

    def far_place(r):
        return (r // W_ROWS) * bins + (r & (bins - 1))

    def far_local(r):
        return W_ROWS // bins - 1 - (r & (W_ROWS - 1)) // bins

    r, w = iota(valid_far_ref.shape, 0), iota(valid_far_ref.shape, 1)
    valid_far_ref[...] = onehot(far_local(w) == at.local(r))
    w, r = iota(spread1_far_ref.shape, 0), iota(spread1_far_ref.shape, 1)
    spread1_far_ref[...] = onehot((far_place(w) == at.place(r)) & (far_local(w) == at.local(r)))
    w, r = iota(spread2_far_ref.shape, 0), iota(spread2_far_ref.shape, 1)
    spread2_far_ref[...] = onehot(far_place(w) == (at.block(r) ^ at.chip ^ at.side))

    row, col = iota(chosen_ref.shape, 0), iota(chosen_ref.shape, 1)
    chosen_ref[...] = onehot(
        (at.block(col) == ((at.side + (row & (bins - 1))) ^ at.chip))
        & (at.place(col) == at.chip)
        & (at.frame(row) == at.frame(col))
    )


def x_rows_of(own):
    return (3 * own + W_ROWS,) * 2 + (3 * own,) * 2


def mixing(refs, devices, own, order, factors, selections, keep2):
    valid_ref, pick1_ref, spread1_ref, keep1_ref, pick2_ref, spread2_ref = selections
    tiles = tiles_of(refs, x_rows_of(own), devices, own, order)
    picked = [
        mul(pick[...], factors, NT).astype(bf16) * valid_ref[...] for pick in (pick1_ref, pick2_ref)
    ]
    mix1 = mul(picked[0], spread1_ref[...]).astype(bf16) * keep1_ref[...]
    mix2 = mul(picked[1], spread2_ref[...]).astype(bf16) * keep2
    return tiles, mul(mix1, jnp.concatenate(tiles, 1)).astype(bf16), mix2


def near_kernel(
    x0, x1, valid_ref, pick1_ref, spread1_ref, keep1_ref, pick2_ref, spread2_ref, keep2_ref,
    first_ref, mix2_ref, part_ref, own_ref, mark_ref,
):
    own = own_ref.shape[0] // 2
    half, rows = mix2_ref.shape
    devices = rows // own
    selections = (valid_ref, pick1_ref, spread1_ref, keep1_ref, pick2_ref, spread2_ref)
    order = halves_of(devices)[0]
    factors = [piece((x0, x1), x_rows_of(own), devices, j, 3 * own, W_ROWS) for j in order]
    tiles, first, mix2 = mixing(
        (x0, x1), devices, own, order, jnp.concatenate(factors, 0), selections, keep2_ref[:half, :]
    )
    first_ref[...] = first
    mix2_ref[...] = mix2
    part_ref[...] = mul(mix2[:, :half], first)
    own_ref[:own, :], own_ref[own:, :] = unpacked(*[tile[:own] for tile in tiles])
    mark_ref[...] = jnp.zeros_like(mark_ref)


def mix_kernel(
    x2, x3, x0, x1, first_near_ref, mix2_near_ref, part_ref,
    valid_ref, pick1_ref, spread1_ref, keep1_ref,
    pick2_ref, spread2_ref, keep2_ref,
    sp_ref, back_ref, sp_own_ref, first_far_ref, mark_ref,
):
    own = sp_own_ref.shape[0] // 2
    half, rows = mix2_near_ref.shape
    devices = rows // own
    selections = (valid_ref, pick1_ref, spread1_ref, keep1_ref, pick2_ref, spread2_ref)
    at_end = (devices // 4 - 1) * 3 * own
    factors = jnp.concatenate([ref[at_end : at_end + W_ROWS, :] for ref in (x2, x3)], 0)
    _, first_far, mix2_far = mixing(
        (x0, x1, x2, x3), devices, own, halves_of(devices)[1], factors, selections, keep2_ref[half:, :]
    )
    first = jnp.concatenate([first_near_ref[...], first_far], 0)
    spectral = jnp.concatenate(
        [
            (part_ref[...] + mul(mix2_near_ref[:, half:], first_far)).astype(bf16),
            mul(mix2_far, first).astype(bf16),
        ],
        0,
    )
    back_ref[:half, :] = mix2_near_ref[:, : 2 * own]
    back_ref[half:, :] = mix2_far[:, : 2 * own]
    sp_low, sp_high = unpacked(*cut(spectral))
    sp_own_ref[:own, :], sp_own_ref[own:, :] = sp_low[:own], sp_high[:own]
    first_far_ref[...] = first_far
    sp_ref[:rows, :] = sp_low
    sp_ref[rows:, :] = sp_high
    mark_ref[...] = jnp.zeros_like(mark_ref)


def hidden_kernel(
    sp_ref, w_in_ref, first_near_ref, first_far_ref, chosen_ref,
    hid_ref, slope_ref, spt_ref, first_ref,
):
    own, half = chosen_ref.shape[0], first_near_ref.shape[0]
    first = mul(chosen_ref[:, :half], first_near_ref[...])
    first += mul(chosen_ref[:, half:], first_far_ref[...])
    first_ref[:own, :], first_ref[own:, :] = unpacked(*cut(first.astype(bf16)))
    sp = sp_ref[...]
    gelu_out, slope = gelu_and_slope(mul(sp, w_in_ref[...]))
    hid_ref[...] = gelu_out.astype(bf16)
    slope_ref[...] = slope
    spt_ref[...] = sp.T


def backward_kernel(
    hid_ref, slope_ref, spt_ref, first_ref, back_ref, sp_own_ref, own_ref, d2, d0, d1, d3,
    s_ref, w_in_t_ref, w_out_ref,
    enh_ref, g1_ref, g2_ref, gwi_ref, gwo_ref,
):
    bins, block = g1_ref.shape
    frames, _, channels = s_ref.shape
    half_c = channels // 2
    own = own_ref.shape[0] // 2
    refs = (d0, d1, d2, d3)
    rows = hid_ref.shape[0] // 2
    devices = rows // own
    at = Rows(own, bins, rows)
    order = sum(halves_of(devices), [])
    dm_low, dm_high = unpacked(*tiles_of(refs, (3 * own,) * 4, devices, own, order))
    sp_own = sp_own_ref[...]
    hidden = jnp.concatenate([hid_ref[:own, :], hid_ref[rows : rows + own, :]], 0)
    mask = (sp_own.astype(f32) + mul(hidden, w_out_ref[...], NT)).astype(bf16).astype(f32)
    spec = s_ref[...].astype(f32).reshape(2 * own, channels)
    spec_re, spec_im = spec[:, :half_c], spec[:, half_c:]
    mask_re, mask_im = mask[:, :half_c], mask[:, half_c:]
    enhanced = jnp.concatenate(
        [spec_re * mask_re - spec_im * mask_im, spec_re * mask_im + spec_im * mask_re], 1
    )
    enh_ref[...] = enhanced.reshape(frames, bins, channels).astype(bf16)

    parts = 2 * rows // 4
    dm = [half[k : k + parts] for half in (dm_low, dm_high) for k in range(0, rows, parts)]
    dpre, dsp = [], []
    for n, part in enumerate(dm):
        to = slice(n * parts, (n + 1) * parts)
        dpre.append((mul(part, w_out_ref[...]) * slope_ref[to, :]).astype(bf16))
        dsp.append((part.astype(f32) + mul(dpre[n], w_in_t_ref[...])).astype(bf16))
    dpre, dsp = jnp.concatenate(dpre, 0), jnp.concatenate(dsp, 0)
    dsp = dsp[:rows], dsp[rows:]
    gwi_ref[...] = mul(spt_ref[...], dpre)
    gwo_ref[...] = mul(jnp.concatenate([dm_low, dm_high], 0), hid_ref[...], TN)

    dsp_low, dsp_high = dsp
    dfirst_low = mul(back_ref[...], dsp_low, TN).astype(bf16)
    dfirst_high = mul(back_ref[...], dsp_high, TN).astype(bf16)

    per_block = at.per_block
    frames_meet = at.frame(iota((own, per_block), 0)) == at.frame(iota((own, per_block), 1))

    def bin_sums(gram):
        parts = jnp.where(frames_meet, gram, 0.0)
        total = sum(parts[n : n + 2 * bins] for n in range(0, own, 2 * bins))
        return total[:bins] + total[bins:]

    gram = mul(own_ref[:own, :], dfirst_low, NT) + mul(own_ref[own:, :], dfirst_high, NT)
    sums = [bin_sums(gram)]
    gram = mul(first_ref[:own, :], dsp_low[:per_block], NT)
    gram += mul(first_ref[own:, :], dsp_high[:per_block], NT)
    sums.append(bin_sums(gram))
    row, col = iota((2 * per_block, 2 * block), 0), iota((2 * per_block, 2 * block), 1)
    place = at.place(row & (per_block - 1))
    take = ((row < per_block) & (place == col)) | (
        (row >= per_block) & (block + (place ^ at.side) == col)
    )
    left, both, chosen = jnp.concatenate(sums, 1), 0.0, onehot(take)
    for _ in range(3):
        part = left.astype(bf16)
        both += mul(part, chosen)
        left -= part.astype(f32)
    g1_ref[...] = both[:, :block]
    g2_ref[...] = both[:, block:]


def whole_rows(features, spectrum, cotangent, w_first, w_second, w_in, w_out):
    frames, bins, channels = features.shape
    block = w_first.shape[1]
    hid = w_in.shape[1]
    devices = lax.axis_size("freq")
    own = frames // 2 * bins
    rows = devices * own
    in_vmem = lambda n: [pl.BlockSpec(memory_space=pltpu.VMEM)] * n
    in_hbm = lambda n: [pl.BlockSpec(memory_space=pltpu.HBM)] * n
    shaped = jax.ShapeDtypeStruct
    params = pltpu.CompilerParams(vmem_limit_bytes=40 * 2**20)
    scale = 1.0 / math.sqrt(frames * devices * bins)
    own_rows, spec_in, w_in_in, w_out_in = pl.pallas_call(
        functools.partial(pack_kernel, scale=scale),
        out_shape=(
            pltpu.VMEM((6 * own + W_ROWS, LANES), bf16),
            pltpu.VMEM((frames, bins, channels), bf16),
            pltpu.VMEM((channels, hid), bf16),
            pltpu.VMEM((channels, hid), bf16),
        ),
        in_specs=in_hbm(7),
        out_specs=tuple(in_vmem(4)),
        scratch_shapes=[
            pltpu.VMEM((frames, bins, channels), bf16),
            pltpu.VMEM((frames, bins, channels), bf16),
            pltpu.VMEM((bins, block), bf16),
            pltpu.VMEM((bins, block), bf16),
            pltpu.SemaphoreType.DMA((7,)),
        ],
        name="pack",
    )(features, spectrum, cotangent, w_first, w_second, w_in, w_out.T)
    w_rows = devices * W_ROWS
    x_own, d_own, w_in_t, *selections = pl.pallas_call(
        functools.partial(prepare_kernel, bins=bins),
        out_shape=tuple(
            pltpu.VMEM(shape, bf16)
            for shape in [
                (3 * own + W_ROWS, LANES),
                (3 * own, LANES),
                (hid, channels),
                (rows // 2, w_rows // 2),
                (rows // 2, LANES),
                (w_rows // 2, rows // 2),
                (rows // 2, rows // 2),
                (rows // 2, LANES),
                (w_rows // 2, rows),
                (rows, rows),
                (rows // 2, 2 * W_ROWS),
                (2 * W_ROWS, rows // 2),
                (2 * W_ROWS, rows),
                (own, rows),
            ]
        ),
        in_specs=in_vmem(2),
        out_specs=tuple(in_vmem(14)),
        compiler_params=params,
        cost_estimate=pl.CostEstimate(flops=0, bytes_accessed=2**21, transcendentals=0),
        name="prepare",
    )(own_rows, w_in_in)

    column = [exchanged(own_rows, j) for j in range(devices - 4, 0, -4)]
    x_rows = 3 * own + W_ROWS
    across = exchanged(own_rows, 2)
    sent = [*column, own_rows]
    x_column = jnp.concatenate(
        [got[: 3 * own] for got in column]
        + [got[3 * own : 3 * own + bins] for got in sent],
        0,
    )
    d_column = jnp.concatenate([got[x_rows:] for got in column], 0)
    x2, d2 = exchanged(x_column, 2), exchanged(d_column, 2)
    x0 = jnp.concatenate([*[got[:x_rows] for got in column], x_own, across[:x_rows]], 0)
    d0 = jnp.concatenate([d_column, d_own, across[x_rows:]], 0)
    x1, d1 = exchanged(x0, 1), exchanged(d0, 1)
    first_near, mix2_near, part, x_rows_own, mark = pl.pallas_call(
        near_kernel,
        out_shape=(
            pltpu.VMEM((rows // 2, 2 * channels), bf16),
            pltpu.VMEM((rows // 2, rows), bf16),
            pltpu.VMEM((rows // 2, 2 * channels), f32),
            pltpu.VMEM((2 * own, channels), bf16),
            pltpu.VMEM((W_ROWS, LANES), bf16),
        ),
        in_specs=in_vmem(9),
        out_specs=tuple(in_vmem(5)),
        compiler_params=params,
        name="near",
    )(x0, x1, *selections[:7])
    x3 = exchanged(jnp.concatenate([x2, mark], 0), 1)
    pick1, keep1, pick2, keep2 = (selections[n] for n in (1, 3, 4, 6))
    valid_far, spread1_far, spread2_far = selections[7:10]
    spectral, *kept, first_far, mark = pl.pallas_call(
        mix_kernel,
        out_shape=tuple(
            pltpu.VMEM(shape, bf16)
            for shape in [
                (2 * rows, channels),
                (rows, 2 * own),
                (2 * own, channels),
                (rows // 2, 2 * channels),
                (W_ROWS, LANES),
            ]
        ),
        in_specs=in_vmem(14),
        out_specs=tuple(in_vmem(5)),
        compiler_params=params,
        name="mix",
    )(
        x2, x3, x0, x1, first_near, mix2_near, part,
        valid_far, pick1, spread1_far, keep1, pick2, spread2_far, keep2,
    )
    d3 = exchanged(jnp.concatenate([d2, mark], 0), 1)
    hidden = pl.pallas_call(
        hidden_kernel,
        out_shape=(
            pltpu.VMEM((2 * rows, hid), bf16),
            pltpu.VMEM((2 * rows, hid), f32),
            pltpu.VMEM((channels, 2 * rows), bf16),
            pltpu.VMEM((2 * own, channels), bf16),
        ),
        in_specs=in_vmem(5),
        out_specs=tuple(in_vmem(4)),
        compiler_params=params,
        name="hidden",
    )(spectral, w_in_in, first_near, first_far, selections[-1])

    enhanced, grad_first, grad_second, grad_w_in, grad_w_out = pl.pallas_call(
        backward_kernel,
        out_shape=(
            shaped((frames, bins, channels), bf16),
            shaped((bins, block), f32),
            shaped((bins, block), f32),
            shaped((channels, hid), f32),
            shaped((channels, hid), f32),
        ),
        in_specs=in_vmem(14),
        out_specs=tuple(in_vmem(5)),
        compiler_params=params,
        name="backward",
    )(*hidden, *kept, x_rows_own, d2, d0, d1, d3, spec_in, w_in_t, w_out_in)
    return enhanced, grad_first, grad_second, grad_w_in, grad_w_out.T


def exchanged(value, mask):
    pairs = [(source, source ^ mask) for source in range(lax.axis_size("freq"))]
    return lax.ppermute(value, "freq", pairs)


def on_device(features, spectrum, cotangent, w_first, w_second, w_in, w_out):
    frames, bins, channels = features.shape
    block = w_first.shape[1]
    devices = lax.axis_size("freq")
    gathered_bytes = 2 * 2 * devices * frames * bins * channels
    fits = gathered_bytes <= 4 * 2**20
    shaped = (
        block == 2 * bins
        and devices == 2 * block
        and bins <= W_ROWS
        and 2 * block <= LANES
        and LANES < channels
        and 2 * (channels - LANES) == LANES
        and devices % 4 == 0
        and devices // 4 * bins == W_ROWS
    )
    plan = whole_rows if fits and shaped else split_rows
    return plan(features, spectrum, cotangent, w_first, w_second, w_in, w_out)


def solution(mesh):
    placed = (
        P("groups", "freq", None),
        P("groups", "freq", None),
        P("groups", "freq", None),
        P("freq", None),
        P("freq", None),
        P(),
        P(),
    )
    return jax.shard_map(
        on_device,
        mesh=mesh,
        in_specs=placed,
        out_specs=(
            P("groups", "freq", None),
            P("freq", "groups"),
            P("freq", "groups"),
            P("groups", None),
            P("groups", None),
        ),
        check_vma=False,
    )
```
